128 devices in a mesh: dp: 64 (over x, z, y), tensor: 2 (over core).
Axes of the slice: x: 4, y: 4, z: 4, core: 2. Of those that a mesh axis runs over, the one named last changes fastest.
Arguments:
- latent_kv: bfloat16 [32768, 512], P('dp', 'tensor'), may hold values from -6 to 6
- latent_q: bfloat16 [32768, 1536], P('dp', 'tensor'), may hold values from -6 to 6
- grad_kv: bfloat16 [32768, 8192], P('dp'), may hold values from -0.09375 to 0.09375
- grad_q: bfloat16 [32768, 6144], P('dp'), may hold values from -0.09375 to 0.09375
- momentum_kv: float32 [8192, 512], P('dp', 'tensor'), may hold values from -20 to 20
- momentum_q: float32 [6144, 1536], P('dp', 'tensor'), may hold values from -20 to 20
Outputs:
- update_kv: bfloat16 [8192, 512], P('dp', 'tensor')
- momentum_kv_new: float32 [8192, 512], P('dp', 'tensor')
- update_q: bfloat16 [6144, 1536], P('dp', 'tensor')
- momentum_q_new: float32 [6144, 1536], P('dp', 'tensor')
The draws below stay inside these ranges and needn't reach their ends.
All inputs are finite; a program needn't handle non-finite values.
Results may differ from the reference program's by a relative error of at most 0.035.
Values may be sent and summed in bfloat16 or wider, within the bound.
A program may use at most 256 MiB of HBM per device.

```python
import jax
import jax.numpy as jnp
from jax import lax

KV_RANK = 512
Q_RANK = 1536
KV_OUT = 256
Q_OUT = 192
ITERS = 5
HEADS = 32
TOKENS = 32768


def scaled_entries(seed_key, base_values, ramp_top):
    row_key, col_key = jax.random.split(seed_key)
    rows_count, cols_count = base_values.shape
    row_scale = 10.0 ** jax.random.uniform(row_key, (rows_count, 1))
    position = jnp.arange(cols_count, dtype=jnp.float32).reshape(1, cols_count) / (cols_count - 1)
    col_scale = ramp_top ** position * 2.0 ** jax.random.uniform(col_key, (1, cols_count))
    return (0.05 * base_values * row_scale * col_scale).astype(jnp.float32)


def draw_momentum_kv(seed_key, part_index):
    seed_key = jax.random.fold_in(seed_key, 11)
    scale_key, value_key = jax.random.split(seed_key)
    shape_pair = (HEADS * KV_OUT, KV_RANK)
    base_values = jnp.clip(jax.random.normal(value_key, shape_pair), -2.0, 2.0)
    ramp_top = 10.0
    return scaled_entries(scale_key, base_values, ramp_top)


def draw_momentum_q(seed_key, part_index):
    seed_key = jax.random.fold_in(seed_key, 23)
    scale_key, value_key = jax.random.split(seed_key)
    shape_pair = (HEADS * Q_OUT, Q_RANK)
    base_values = jnp.clip(jax.random.normal(value_key, shape_pair), -2.0, 2.0)
    ramp_top = 10.0
    return scaled_entries(scale_key, base_values, ramp_top)


def strengthened(array, rng, source, target, blocks, factor):
    def block_of(axis_at):
        return (jnp.arange(array.shape[axis_at]) // (array.shape[axis_at] // blocks)).reshape((-1,) + (1,) * (array.ndim - 1 - axis_at))

    first = jax.random.permutation(rng, blocks)[block_of(target)]
    other_side = (block_of(target) + blocks // 2) % blocks
    return jnp.where((block_of(source) == first) | (block_of(source) == other_side), factor * array, array)


def shard_levels(own_key, extent, shards, smallest, high):
    def one(axis_at, blocks):
        steps = jax.random.uniform(jax.random.fold_in(jax.random.fold_in(own_key, 6), axis_at), (blocks,), jnp.float32, smallest / len(shards), high / len(shards))
        return jnp.repeat(jnp.exp(steps), extent[axis_at] // blocks).reshape((-1,) + (1,) * (len(extent) - axis_at - 1))

    factor_of = one(*shards[0])
    for cut in shards[1:]:
        factor_of = factor_of * one(*cut)
    return factor_of


def gaussian(key, dims, spread, most, cuts=(), held_as=jnp.bfloat16):
    result = jax.random.normal(key, dims, jnp.float32) * spread
    if len(cuts) > 0:
        result = shard_levels(key, dims, cuts, -0.22, 0.18) * result
    return jnp.clip(result, min=-most, max=most).astype(held_as)


def noise_with(key, extent, width, most, cuts, heavy, kind=jnp.bfloat16):
    result = width * jax.random.normal(key, extent, jnp.float32)
    if cuts:
        result = result * shard_levels(key, extent, cuts, -0.22, 0.18)
    return jnp.clip(strengthened(result, jax.random.fold_in(key, 3), *heavy), -most, most).astype(kind)


def setup_inputs(seed: int = 0) -> dict:
    key_list = jax.random.split(jax.random.key(seed), 7)
    latent_kv = gaussian(key_list[0], (TOKENS, KV_RANK), 1.0, 6.0, ((0, 64), (1, 2)))
    latent_q = gaussian(key_list[1], (TOKENS, Q_RANK), 1.0, 6.0, ((0, 64), (1, 2)))
    grad_kv = noise_with(key_list[2], (TOKENS, HEADS * KV_OUT), TOKENS ** -0.5, 0.09375, ((0, 64),), (0, 1, 64, 4.0))
    grad_q = noise_with(key_list[3], (TOKENS, HEADS * Q_OUT), TOKENS ** -0.5, 0.09375, ((0, 64),), (0, 1, 64, 4.0))
    momentum_kv = draw_momentum_kv(jax.random.fold_in(key_list[6], 71), 0)
    momentum_q = draw_momentum_q(jax.random.fold_in(key_list[6], 71), 0)
    return dict(latent_kv=latent_kv, latent_q=latent_q, grad_kv=grad_kv, grad_q=grad_q, momentum_kv=momentum_kv, momentum_q=momentum_q)


first_coef = 3.4445
second_coef = -4.775
third_coef = 2.0315
momentum_rate = 0.95
norm_eps = 1e-07

def rounded(values):
    low = lax.optimization_barrier(values.astype(jnp.bfloat16))
    return low.astype(jnp.float32)

def orthogonalize(prepared):
    norms = jnp.sqrt(lax.optimization_barrier(jnp.sum(prepared * prepared, axis=(1, 2), keepdims=True)))
    iterate = (prepared / (norms + norm_eps)).astype(jnp.bfloat16)
    for sweep in range(ITERS):
        wide = iterate.astype(jnp.float32)
        gram = rounded(jnp.einsum('hrc,hsc->hrs', wide, wide, precision=lax.Precision.HIGHEST))
        square = jnp.einsum('hrs,hst->hrt', gram, gram, precision=lax.Precision.HIGHEST)
        mixing = rounded(second_coef * gram + third_coef * square)
        moved = jnp.einsum('hrs,hsc->hrc', mixing, wide, precision=lax.Precision.HIGHEST)
        iterate = (first_coef * wide + moved).astype(jnp.bfloat16)
    return iterate

def branch_step(grads, latents, momentum, head_rows):
    heads_count = grads.shape[1] // head_rows
    gradient = jnp.dot(grads.T, latents, preferred_element_type=jnp.float32)
    renewed = momentum_rate * momentum + gradient
    prepared = gradient + momentum_rate * renewed
    shaped = prepared.reshape(heads_count, head_rows, prepared.shape[1])
    update = orthogonalize(shaped).reshape(heads_count * head_rows, prepared.shape[1])
    return (update, renewed)

def reference(latent_kv, latent_q, grad_kv, grad_q, momentum_kv, momentum_q):
    update_kv, renewed_kv = branch_step(grad_kv, latent_kv, momentum_kv, KV_OUT)
    update_q, renewed_q = branch_step(grad_q, latent_q, momentum_q, Q_OUT)
    return (update_kv, renewed_kv, update_q, renewed_q)
```

```python
import functools

import jax
import jax.numpy as jnp
from jax import lax
from jax.experimental import pallas as pl
from jax.experimental.pallas import tpu as pltpu
from jax.sharding import PartitionSpec as P

ITERS = 5
SIDE = 4
MESH = pl.DeviceIdType.MESH

first_coef = 3.4445
second_coef = -4.775
third_coef = 2.0315
momentum_rate = 0.95
norm_eps = 1e-07

TOK = 512
KV_ROWS, KV_COLS = 128, 256
Q_ROWS, Q_COLS = 96, 768
KV_CUT = ((0, 48), (48, 48), (96, 32))
SLAB = 256
ORDERS = ("xzy", "zyx", "yxz")


def shifted(where, axis, step):
    moved = dict(where)
    moved[axis] = lax.rem(moved[axis] + step + SIDE, SIDE)
    return (moved["x"] * SIDE + moved["z"]) * SIDE + moved["y"]


def gram_of(matrix):
    return lax.dot_general(
        matrix, matrix, (((1,), (1,)), ((), ())), preferred_element_type=jnp.float32
    )


def mixer(matrix):
    gram_low = gram_of(matrix).astype(jnp.bfloat16)
    square = jnp.dot(gram_low, gram_low, preferred_element_type=jnp.float32)
    return (second_coef * gram_low.astype(jnp.float32) + third_coef * square).astype(jnp.bfloat16)


def advance(iterate, mixing, source):
    moved = jnp.dot(mixing, source, preferred_element_type=jnp.float32)
    return (first_coef * iterate.astype(jnp.float32) + moved).astype(jnp.bfloat16)


def add_into(target, others, count):
    def step(i, carry):
        total = target[i].astype(jnp.float32)
        for other in others:
            total += other[i].astype(jnp.float32)
        target[i] = total.astype(target.dtype)
        return carry

    lax.fori_loop(0, count, step, 0)


def kernel(
    lat_kv, lat_q, grad_kv, grad_q, mom_kv, mom_q,
    up_kv, new_kv, up_q, new_q,
    lk, lq, gk, gq, part_k, part_q, one_k, one_q, two_k, two_q, three_k, three_q,
    sum_k, sum_q, x_k, x_q, mix_k, mix_q,
    in_sem, gk_sem, gq_sem, send_sem, recv_sem, ag_send, ag_recv,
):
    me = lax.axis_index("dp")
    core = lax.axis_index("tensor")
    where = {"x": me // 16, "z": lax.rem(me // 4, 4), "y": lax.rem(me, 4)}
    low = lax.rem(me, 2)
    twin = me + 1 - 2 * low
    group = ((me, 1 - core), (twin, core), (twin, 1 - core))

    def unit(xr, zr):
        return lax.rem(where["x"] + xr, 4) * 4 + lax.rem(where["z"] + zr, 4)

    def fetch(source, target, sems, width, i):
        at = pl.multiple_of(unit(i // 4, lax.rem(i, 4)) * width, 128)
        return pltpu.make_async_copy(source.at[:, pl.ds(at, width)], target.at[i], sems.at[i])

    fetch_q = functools.partial(fetch, grad_q, gq, gq_sem, 4 * Q_ROWS)
    fetch_k = functools.partial(fetch, grad_kv, gk, gk_sem, 4 * KV_ROWS)
    load_lq = pltpu.make_async_copy(lat_q, lq, in_sem.at[0])
    load_lk = pltpu.make_async_copy(lat_kv, lk, in_sem.at[1])
    load_lq.start()

    def begin(which, i, carry):
        which(i).start()
        return carry

    for row in (2, 3, 1, 0):
        lax.fori_loop(row * 4, row * 4 + 4, functools.partial(begin, fetch_q), 0)
    load_lk.start()
    for row in (2, 3, 1, 0):
        lax.fori_loop(row * 4, row * 4 + 4, functools.partial(begin, fetch_k), 0)

    barrier = pltpu.get_barrier_semaphore()
    friends = [(shifted(where, a, s), core) for a in "xyz" for s in (1, 2, 3)]
    friends += [group[0], group[2]]
    for friend in friends:
        pl.semaphore_signal(barrier, inc=1, device_id=friend, device_id_type=MESH)
    pl.semaphore_wait(barrier, len(friends))

    started = []

    def send(chunk, s, slot, source, target, axis, step):
        copy = pltpu.make_async_remote_copy(
            src_ref=source,
            dst_ref=target,
            send_sem=send_sem.at[chunk, s, slot],
            recv_sem=recv_sem.at[chunk, s, slot],
            device_id=(shifted(where, axis, step), core),
            device_id_type=MESH,
        )
        copy.start()
        started.append(copy)
        return copy

    class Chunk:
        def __init__(self, index, parts, ones, twos, threes):
            self.index, self.parts, self.ones = index, parts, ones
            self.twos, self.threes = twos, threes
            self.copies = {}

        def go(self, s, slot, source, target, axis, step):
            self.copies[s, slot] = send(self.index, s, slot, source, target, axis, step)

        def one_far(self, s):
            part, got, axis = self.parts[s], self.ones[s], ORDERS[s][0]
            self.go(s, 0, part.at[2, pl.ds(0, 2)], got.at[0], axis, 1)
            self.go(s, 1, part.at[2, pl.ds(2, 2)], got.at[1], axis, -1)

        def one_up(self, s):
            part, got, axis = self.parts[s], self.ones[s], ORDERS[s][0]
            self.go(s, 2, part.at[1, pl.ds(2, 2)], got.at[2], axis, 1)

        def one_down(self, s):
            part, got, axis = self.parts[s], self.ones[s], ORDERS[s][0]
            self.go(s, 3, part.at[3, pl.ds(0, 2)], got.at[3], axis, -1)

        def one_relay(self, s):
            part, got, axis = self.parts[s], self.ones[s], ORDERS[s][0]
            self.copies[s, 0].wait_recv()
            for b in range(2):
                add_into(part.at[1, b], [got.at[0, b]], 4)
            self.go(s, 4, part.at[1, pl.ds(0, 2)], got.at[4], axis, 1)
            self.copies[s, 1].wait_recv()
            for b in range(2):
                add_into(part.at[3, 2 + b], [got.at[1, b]], 4)
            self.go(s, 5, part.at[3, pl.ds(2, 2)], got.at[5], axis, -1)

        def one_end_two_begin(self, s):
            part, got, axis = self.parts[s], self.ones[s], ORDERS[s][1]
            two = self.twos[s]
            self.copies[s, 2].wait_recv()
            self.copies[s, 5].wait_recv()
            for b in (2, 3):
                add_into(part.at[0, b], [got.at[2, b - 2], got.at[5, b - 2]], 4)
                self.go(s, 4 + b, part.at[0, b], two.at[b - 1], axis, b)
            self.copies[s, 3].wait_recv()
            self.copies[s, 4].wait_recv()
            for b in (1, 0):
                add_into(part.at[0, b], [got.at[3, b], got.at[4, b]], 4)
                if b == 1:
                    self.go(s, 8, part.at[0, 1], two.at[0], axis, 1)

        def two_end_three_begin(self, s):
            part, two, three = self.parts[s], self.twos[s], self.threes[s]
            for slot in (6, 7, 8):
                self.copies[s, slot].wait_recv()
            add_into(part.at[0, 0], [two.at[0], two.at[1], two.at[2]], 4)
            for c in (1, 2, 3):
                self.go(s, 8 + c, part.at[0, 0, c], three.at[c - 1], ORDERS[s][2], c)

        def three_end(self, s):
            part, three = self.parts[s], self.threes[s]
            for slot in (9, 10, 11):
                self.copies[s, slot].wait_recv()
            total = part[0, 0, 0].astype(jnp.float32)
            for c in range(3):
                total += three[c].astype(jnp.float32)
            return total

    chunk_q = Chunk(0, part_q, one_q, two_q, three_q)
    chunk_k = Chunk(1, part_k, one_k, two_k, three_k)

    def place_of(xr, zr, yr):
        at = {"x": xr, "z": zr, "y": yr}
        return [tuple(at[a] for a in order) for order in ORDERS]

    def unit_q(i, carry):
        fetch_q(i).wait()
        xr, zr = i // 4, lax.rem(i, 4)
        term = lax.dot_general(
            gq[i], lq[...], (((0,), (0,)), ((), ())), preferred_element_type=jnp.float32
        ).astype(jnp.bfloat16)
        for y in range(4):
            yr = lax.rem(y - where["y"] + 4, 4)
            for s, place in enumerate(place_of(xr, zr, yr)):
                part_q[s][place] = term[y * Q_ROWS:(y + 1) * Q_ROWS, s * SLAB:(s + 1) * SLAB]
        return carry

    def unit_k(i, carry):
        fetch_k(i).wait()
        xr, zr = i // 4, lax.rem(i, 4)
        term = lax.dot_general(
            gk[i], lk[...], (((0,), (0,)), ((), ())), preferred_element_type=jnp.float32
        ).astype(jnp.bfloat16)
        for y in range(4):
            yr = lax.rem(y - where["y"] + 4, 4)
            for s, place in enumerate(place_of(xr, zr, yr)):
                at, rows = KV_CUT[s]
                part_k[s][place] = term[y * KV_ROWS + at:y * KV_ROWS + at + rows]
        return carry

    load_lq.wait()
    lax.fori_loop(8, 12, unit_q, 0)
    chunk_q.one_far(0)
    lax.fori_loop(12, 16, unit_q, 0)
    chunk_q.one_down(0)
    lax.fori_loop(4, 8, unit_q, 0)
    chunk_q.one_up(0)
    lax.fori_loop(0, 4, unit_q, 0)
    for s in (1, 2):
        chunk_q.one_far(s)
        chunk_q.one_down(s)
        chunk_q.one_up(s)

    load_lk.wait()
    lax.fori_loop(0, 16, unit_k, 0)

    for s in range(3):
        chunk_q.one_relay(s)
    for s in range(3):
        chunk_k.one_far(s)
        chunk_k.one_down(s)
        chunk_k.one_up(s)
    for s in range(3):
        chunk_q.one_end_two_begin(s)
    for s in range(3):
        chunk_k.one_relay(s)
    for s in range(3):
        chunk_q.two_end_three_begin(s)
    for s in range(3):
        chunk_k.one_end_two_begin(s)

    def gather(chunk, x_ref, rows, cols):
        def slot(owner, c):
            return x_ref.at[
                pl.ds(pl.multiple_of(lax.rem(owner, 2) * rows, rows), rows),
                pl.ds(pl.multiple_of(c * cols, cols), cols),
            ]

        mine = slot(me, core)
        copies = []
        for k, (owner, c) in enumerate(group):
            copies.append(
                pltpu.make_async_remote_copy(
                    src_ref=mine,
                    dst_ref=mine,
                    send_sem=ag_send.at[chunk, k],
                    recv_sem=ag_recv.at[chunk, k],
                    device_id=(owner, c),
                    device_id_type=MESH,
                )
            )
            copies[-1].start()

        def finish():
            for k, (owner, c) in enumerate(group):
                pltpu.make_async_remote_copy(
                    src_ref=mine,
                    dst_ref=slot(owner, c),
                    send_sem=ag_send.at[chunk, k],
                    recv_sem=ag_recv.at[chunk, k],
                    device_id=(owner, c),
                    device_id_type=MESH,
                ).wait_recv()
            for copy in copies:
                copy.wait_send()

        return finish

    def own_rows(rows):
        return pl.ds(pl.multiple_of(low * rows, rows), rows)

    def own_cols(cols):
        return pl.ds(pl.multiple_of(core * cols, cols), cols)

    def prepare(gradient, held, new_ref, x_ref, rows, cols):
        renewed = momentum_rate * held[...] + gradient
        new_ref[...] = renewed
        prepared = gradient + momentum_rate * renewed
        x_ref[own_rows(rows), own_cols(cols)] = prepared.astype(jnp.bfloat16)

    def newton(x_ref, mix_ref, out_ref, rows, cols):
        wide = x_ref[...].astype(jnp.float32)
        norm = jnp.sqrt(jnp.sum(wide * wide, keepdims=True)) + norm_eps
        x_ref[...] = (wide / norm).astype(jnp.bfloat16)
        for sweep in range(ITERS - 1):
            whole = x_ref[...]
            x_ref[...] = advance(whole, mixer(whole), whole)
        mix_ref[...] = mixer(x_ref[...])
        out_ref[...] = advance(
            x_ref[own_rows(rows), own_cols(cols)],
            mix_ref[own_rows(rows), :],
            x_ref[:, own_cols(cols)],
        )

    for s in range(3):
        sum_q[:, s * SLAB:(s + 1) * SLAB] = chunk_q.three_end(s)
    prepare(sum_q[...], mom_q, new_q, x_q, Q_ROWS, Q_COLS)
    end_q = gather(0, x_q, Q_ROWS, Q_COLS)

    for s in range(3):
        chunk_k.two_end_three_begin(s)
    end_q()
    newton(x_q, mix_q, up_q, Q_ROWS, Q_COLS)

    for s in range(3):
        at, rows = KV_CUT[s]
        sum_k[at:at + rows, :] = chunk_k.three_end(s)
    prepare(sum_k[...], mom_kv, new_kv, x_k, KV_ROWS, KV_COLS)
    gather(1, x_k, KV_ROWS, KV_COLS)()
    newton(x_k, mix_k, up_kv, KV_ROWS, KV_COLS)

    for copy in started:
        copy.wait_send()


def per_device(latent_kv, latent_q, grad_kv, grad_q, momentum_kv, momentum_q):
    low, full = jnp.bfloat16, jnp.float32
    kv_rows = [rows for _, rows in KV_CUT]
    q_rows = [Q_ROWS] * 3

    def cells(lead, rows_of):
        return [pltpu.VMEM(lead + (rows, SLAB), low) for rows in rows_of]

    vmem = pl.BlockSpec(memory_space=pltpu.VMEM)
    hbm = pl.BlockSpec(memory_space=pl.ANY)
    return pl.pallas_call(
        kernel,
        out_shape=(
            jax.ShapeDtypeStruct((KV_ROWS, KV_COLS), low),
            jax.ShapeDtypeStruct((KV_ROWS, KV_COLS), full),
            jax.ShapeDtypeStruct((Q_ROWS, Q_COLS), low),
            jax.ShapeDtypeStruct((Q_ROWS, Q_COLS), full),
        ),
        in_specs=[hbm, hbm, hbm, hbm, vmem, vmem],
        out_specs=(vmem, vmem, vmem, vmem),
        scratch_shapes=[
            pltpu.VMEM((TOK, KV_COLS), low),
            pltpu.VMEM((TOK, Q_COLS), low),
            pltpu.VMEM((16, TOK, 4 * KV_ROWS), low),
            pltpu.VMEM((16, TOK, 4 * Q_ROWS), low),
            cells((4, 4, 4), kv_rows),
            cells((4, 4, 4), q_rows),
            cells((6, 2, 4), kv_rows),
            cells((6, 2, 4), q_rows),
            cells((3, 4), kv_rows),
            cells((3, 4), q_rows),
            cells((3,), kv_rows),
            cells((3,), q_rows),
            pltpu.VMEM((KV_ROWS, KV_COLS), full),
            pltpu.VMEM((Q_ROWS, Q_COLS), full),
            pltpu.VMEM((2 * KV_ROWS, 2 * KV_COLS), low),
            pltpu.VMEM((2 * Q_ROWS, 2 * Q_COLS), low),
            pltpu.VMEM((2 * KV_ROWS, 2 * KV_ROWS), low),
            pltpu.VMEM((2 * Q_ROWS, 2 * Q_ROWS), low),
            pltpu.SemaphoreType.DMA((2,)),
            pltpu.SemaphoreType.DMA((16,)),
            pltpu.SemaphoreType.DMA((16,)),
            pltpu.SemaphoreType.DMA((2, 3, 12)),
            pltpu.SemaphoreType.DMA((2, 3, 12)),
            pltpu.SemaphoreType.DMA((2, 3)),
            pltpu.SemaphoreType.DMA((2, 3)),
        ],
        compiler_params=pltpu.CompilerParams(
            collective_id=0, has_side_effects=True, vmem_limit_bytes=62 * 2**20
        ),
        name="muon",
    )(latent_kv, latent_q, grad_kv, grad_q, momentum_kv, momentum_q)


def solution(mesh):
    in_specs = (
        P("dp", "tensor"),
        P("dp", "tensor"),
        P("dp", None),
        P("dp", None),
        P("dp", "tensor"),
        P("dp", "tensor"),
    )
    out_specs = (P("dp", "tensor"), P("dp", "tensor"), P("dp", "tensor"), P("dp", "tensor"))
    return jax.shard_map(
        per_device, mesh=mesh, in_specs=in_specs, out_specs=out_specs, check_vma=False
    )
```

```python
import functools

import jax
import jax.numpy as jnp
from jax import lax
from jax.experimental import pallas as pl
from jax.experimental.pallas import tpu as pltpu
from jax.sharding import PartitionSpec as P

ITERS = 5
SIDE = 4
MESH = pl.DeviceIdType.MESH

first_coef = 3.4445
second_coef = -4.775
third_coef = 2.0315
momentum_rate = 0.95
norm_eps = 1e-07

TOK = 512
KV_ROWS, KV_COLS = 128, 256
Q_ROWS, Q_COLS = 96, 768
LANES = 128
SLAB = 2 * LANES
ORDERS = ("xzy", "zyx", "yxz")
KV_CUT = ((0, 48), (48, 48), (96, 32))
Q_CUT = ((0, 96),) * 3
SECOND, THIRD, FOURTH = 6, 12, 15
SLOTS = 17
RINGS = ("q0", "q1")

PLAN = (
    "relay1 q0", "products k", "far k0", "far k1", "near k1", "second q0", "relay1 q1",
    "near k0", "relay1 k0", "relay2 q0", "relay1 k1", "second q1", "third q0", "relay2 q1",
    "second k0", "third q1", "second k1", "third k0", "last q1", "last q0", "gather q",
    "third k1", "last k0", "last k1", "gather k", "forward q", "end q", "end k",
)


def shifted(where, axis, step):
    moved = dict(where)
    moved[axis] = lax.rem(moved[axis] + step + SIDE, SIDE)
    return (moved["x"] * SIDE + moved["z"]) * SIDE + moved["y"]


def gram_of(matrix):
    return lax.dot_general(
        matrix, matrix, (((1,), (1,)), ((), ())), preferred_element_type=jnp.float32
    )


def mixers(grams):
    lows = [gram.astype(jnp.bfloat16) for gram in grams]
    squares = [jnp.dot(low, low, preferred_element_type=jnp.float32) for low in lows]
    return [
        (second_coef * low.astype(jnp.float32) + third_coef * square).astype(jnp.bfloat16)
        for low, square in zip(lows, squares)
    ]


def advance(iterate, mixing, source, scale=None):
    moved = jnp.dot(mixing, source, preferred_element_type=jnp.float32)
    total = first_coef * iterate.astype(jnp.float32) + moved
    if scale is not None:
        total = total * scale
    return total.astype(jnp.bfloat16)


def scale_of(gram):
    at = [lax.broadcasted_iota(jnp.int32, gram.shape, d) for d in range(2)]
    squares = jnp.sum(jnp.where(at[0] == at[1], gram, 0.0), keepdims=True)
    return 1.0 / (jnp.sqrt(squares) + norm_eps)


def newton(heads):
    own_row, own_col = lax.rem(lax.axis_index("dp"), 2), lax.axis_index("tensor")
    for sweep in range(ITERS):
        source = [head[0] if sweep == 0 else head[1] for head in heads]
        wholes = [ref[...] for ref in source]
        grams = [gram_of(whole) for whole in wholes]
        scales = [None] * len(heads)
        if sweep == 0:
            scales = [scale_of(gram) for gram in grams]
            grams = [gram * scale * scale for gram, scale in zip(grams, scales)]
        mixings = mixers(grams)
        for head, whole, mixing, scale in zip(heads, wholes, mixings, scales):
            _, x_ref, mix_ref, out_ref = head
            if sweep < ITERS - 1:
                x_ref[...] = advance(whole, mixing, whole, scale)
                continue
            mix_ref[...] = mixing
            rows, cols = out_ref.shape
            own_rows = pl.ds(pl.multiple_of(own_row * rows, rows), rows)
            own_cols = pl.ds(pl.multiple_of(own_col * cols, cols), cols)
            out_ref[...] = advance(
                x_ref[own_rows, own_cols], mix_ref[own_rows, :], x_ref[:, own_cols]
            )


def add_into(target, others, count):
    def step(i, carry):
        total = target[i].astype(jnp.float32)
        for other in others:
            total += other[i].astype(jnp.float32)
        target[i] = total.astype(target.dtype)
        return carry

    lax.fori_loop(0, count, step, 0)


def kernel(
    lat_kv, lat_q, grad_kv, grad_q, mom_kv, mom_q,
    x_k, x_q, new_k, new_q,
    lk, lq, gk, gq, parts, ones, twos, threes, sum_k, sum_q, held_k, held_q,
    in_sem, gk_sem, gq_sem, send_sem, recv_sem, ag_send, ag_recv,
):
    me = lax.axis_index("dp")
    core = lax.axis_index("tensor")
    where = {"x": me // 16, "z": lax.rem(me // 4, 4), "y": lax.rem(me, 4)}
    low = lax.rem(me, 2)
    twin = me + 1 - 2 * low
    group = ((me, 1 - core), (twin, core), (twin, 1 - core))

    barrier = pltpu.get_barrier_semaphore()
    friends = [(shifted(where, a, s), core) for a in "xyz" for s in (1, 2, 3)]
    friends += [group[0], group[2]]
    for friend in friends:
        pl.semaphore_signal(barrier, inc=1, device_id=friend, device_id_type=MESH)

    def fetch(source, target, sems, width, i):
        u = lax.rem(where["x"] + i // 4, 4) * 4 + lax.rem(where["z"] + lax.rem(i, 4), 4)
        at = pl.multiple_of(u * width, 128)
        return pltpu.make_async_copy(source.at[:, pl.ds(at, width)], target.at[i], sems.at[i])

    fetch_q = functools.partial(fetch, grad_q, gq, gq_sem, 4 * Q_ROWS)
    fetch_k = functools.partial(fetch, grad_kv, gk, gk_sem, 4 * KV_ROWS)
    load_lq = [
        pltpu.make_async_copy(
            lat_q.at[:, pl.ds(k * SLAB, SLAB)], lq.at[:, pl.ds(k * SLAB, SLAB)], in_sem.at[k]
        )
        for k in range(3)
    ]
    load_lk = pltpu.make_async_copy(lat_kv, lk, in_sem.at[3])
    load_held = [
        pltpu.make_async_copy(mom_kv, held_k, in_sem.at[4]),
        pltpu.make_async_copy(mom_q, held_q, in_sem.at[5]),
    ]
    load_lq[0].start()
    for i in (8, 9, 10, 11):
        fetch_q(i).start()
    load_lq[2].start()
    for i in (0, 1, 2, 3):
        fetch_q(i).start()
    load_lq[1].start()
    for i in (6, 14, 12, 13, 15, 4, 5, 7):
        fetch_q(i).start()

    started = []

    class Chunk:
        def __init__(self, index, ring):
            self.index, self.ring = index, ring
            self.parts, self.ones = parts[index], ones[index]
            self.twos, self.threes = twos[index], threes[index]
            self.copies, self.split = {}, set()

        def go(self, s, slot, source, target, axis, step):
            copy = pltpu.make_async_remote_copy(
                src_ref=source,
                dst_ref=target,
                send_sem=send_sem.at[self.index, s, slot],
                recv_sem=recv_sem.at[self.index, s, slot],
                device_id=(shifted(where, axis, step), core),
                device_id_type=MESH,
            )
            copy.start()
            started.append(copy)
            self.copies[s, slot] = copy

        def arrived(self, s, *slots):
            for slot in slots:
                self.copies[s, slot].wait_recv()

        def far(self, s, half):
            part, got, axis = self.parts[s], self.ones[s], ORDERS[s][0]
            step = 1 if half == 0 else -1
            self.go(s, half, part.at[2, pl.ds(2 * half, 2)], got.at[half], axis, step)

        def far_one(self, s, b):
            part, got, axis = self.parts[s], self.ones[s], ORDERS[s][0]
            half, at = b // 2, b % 2
            slot = FOURTH + half if at else half
            step = 1 if half == 0 else -1
            self.go(s, slot, part.at[2, b], got.at[half, at], axis, step)
            self.split.add(s)

        def far_in(self, s, half):
            self.arrived(s, half)
            if s in self.split:
                self.arrived(s, FOURTH + half)

        def near(self, s, half):
            part, got, axis = self.parts[s], self.ones[s], ORDERS[s][0]
            if half == 0:
                self.go(s, 3, part.at[3, pl.ds(0, 2)], got.at[3], axis, -1)
            else:
                self.go(s, 2, part.at[1, pl.ds(2, 2)], got.at[2], axis, 1)

        def relay1(self, s):
            part, got, axis = self.parts[s], self.ones[s], ORDERS[s][0]
            self.far_in(s, 0)
            for b in range(2):
                add_into(part.at[1, b], [got.at[0, b]], 4)
            self.go(s, 4, part.at[1, pl.ds(0, 2)], got.at[4], axis, 1)
            self.far_in(s, 1)
            for b in range(2):
                add_into(part.at[3, 2 + b], [got.at[1, b]], 4)
            self.go(s, 5, part.at[3, pl.ds(2, 2)], got.at[5], axis, -1)

        def second(self, s):
            part, got, two, axis = self.parts[s], self.ones[s], self.twos[s], ORDERS[s][1]
            self.arrived(s, 2, 5)
            add_into(part.at[0, 2], [got.at[2, 0], got.at[5, 0]], 4)
            if self.ring:
                for half, step in ((0, 1), (1, -1)):
                    self.go(
                        s, SECOND + half, part.at[0, 2, pl.ds(2 * half, 2)],
                        two.at[pl.ds(2 * half, 2)], axis, step,
                    )
            else:
                self.go(s, SECOND + 1, part.at[0, 2], two.at[pl.ds(4, 4)], axis, 2)
            add_into(part.at[0, 3], [got.at[2, 1], got.at[5, 1]], 4)
            if self.ring:
                self.go(s, SECOND + 3, part.at[0, 3, pl.ds(0, 2)], two.at[pl.ds(6, 2)], axis, -1)
            else:
                self.go(s, SECOND + 2, part.at[0, 3], two.at[pl.ds(8, 4)], axis, 3)
            self.arrived(s, 3, 4)
            add_into(part.at[0, 1], [got.at[3, 1], got.at[4, 1]], 4)
            if self.ring:
                self.go(s, SECOND + 2, part.at[0, 1, pl.ds(2, 2)], two.at[pl.ds(4, 2)], axis, 1)
            else:
                self.go(s, SECOND, part.at[0, 1], two.at[pl.ds(0, 4)], axis, 1)
            add_into(part.at[0, 0], [got.at[3, 0], got.at[4, 0]], 4)

        def relay2(self, s):
            part, two, axis = self.parts[s], self.twos[s], ORDERS[s][1]
            for half, b, step in ((0, 1, 1), (1, 3, -1)):
                held = part.at[0, b, pl.ds(2 * half, 2)]
                self.arrived(s, SECOND + half)
                add_into(held, [two.at[pl.ds(2 * half, 2)]], 2)
                self.go(
                    s, SECOND + 4 + half, held, two.at[pl.ds(8 + 2 * half, 2)], axis, step
                )

        def third(self, s):
            part, two, three, axis = self.parts[s], self.twos[s], self.threes[s], ORDERS[s][2]
            if self.ring:
                for half, slots in ((0, (3, 4)), (1, (2, 5))):
                    self.arrived(s, *(SECOND + k for k in slots))
                    add_into(
                        part.at[0, 0, pl.ds(2 * half, 2)],
                        [two.at[pl.ds(2 * k, 2)] for k in slots], 2,
                    )
            else:
                self.arrived(s, *(SECOND + k for k in range(3)))
                add_into(part.at[0, 0], [two.at[pl.ds(4 * k, 4)] for k in range(3)], 4)
            for c in (2, 1, 3):
                self.go(s, THIRD - 1 + c, part.at[0, 0, c], three.at[c - 1], axis, c)

        def total(self, s):
            part, three = self.parts[s], self.threes[s]
            self.arrived(s, *(THIRD + k for k in range(3)))
            total = part[0, 0, 0].astype(jnp.float32)
            for c in range(3):
                total += three[c].astype(jnp.float32)
            return total

    chunks = {name: Chunk(at, name in RINGS) for at, name in enumerate(("q0", "q1", "k0", "k1"))}

    def store(pair, cuts, stride, s, i, term, lanes_from):
        xr, zr = i // 4, lax.rem(i, 4)
        at, rows = cuts[s]
        for y in range(4):
            place = {"x": xr, "z": zr, "y": lax.rem(y - where["y"] + 4, 4)}
            place = tuple(place[a] for a in ORDERS[s])
            for half in range(2):
                lane = lanes_from + half * LANES
                chunks[pair[half]].parts[s][place] = term[
                    y * stride + at:y * stride + at + rows, lane:lane + LANES
                ]

    def slab_q(s, unit_of, count):
        def step(j, carry):
            i = unit_of(j)
            term = lax.dot_general(
                gq[i], lq[:, s * SLAB:(s + 1) * SLAB], (((0,), (0,)), ((), ())),
                preferred_element_type=jnp.float32,
            ).astype(jnp.bfloat16)
            store(("q0", "q1"), Q_CUT, Q_ROWS, s, i, term, 0)
            return carry

        lax.fori_loop(0, count, step, 0)

    def unit_k(i, carry):
        fetch_k(i).wait()
        term = lax.dot_general(
            gk[i], lk[...], (((0,), (0,)), ((), ())), preferred_element_type=jnp.float32
        ).astype(jnp.bfloat16)
        for s in range(3):
            store(("k0", "k1"), KV_CUT, KV_ROWS, s, i, term, 0)
        return carry

    q_ready = []

    def need_q(*units):
        for i in units:
            if i not in q_ready:
                q_ready.append(i)
                fetch_q(i).wait()

    def each_q(act, *args):
        for name in ("q0", "q1"):
            getattr(chunks[name], act)(*args)

    load_lq[0].wait()
    need_q(8, 9)
    slab_q(0, lambda j: 8 + j, 2)
    pl.semaphore_wait(barrier, len(friends))
    each_q("far", 0, 0)
    need_q(10, 11)
    slab_q(0, lambda j: 10 + j, 2)
    each_q("far", 0, 1)
    load_lq[2].wait()
    slab_q(2, lambda j: 8 + j, 4)
    each_q("far_one", 2, 2)
    need_q(0, 1, 2, 3)
    slab_q(2, lambda j: j, 4)
    each_q("far_one", 2, 0)
    load_lq[1].wait()
    need_q(6, 14)
    slab_q(1, lambda j: 2 + 4 * j, 4)
    each_q("far", 1, 0)
    each_q("far", 1, 1)
    load_lk.start()
    for i in range(16):
        fetch_k(i).start()
    for load in load_held:
        load.start()
    need_q(12, 13, 15)
    slab_q(2, lambda j: 12 + j, 4)
    each_q("far_one", 2, 3)
    need_q(4, 5, 7)
    slab_q(2, lambda j: 4 + j, 4)
    each_q("far_one", 2, 1)
    slab_q(0, lambda j: 4 + j, 4)
    each_q("near", 0, 1)
    slab_q(0, lambda j: 12 + j, 4)
    each_q("near", 0, 0)
    slab_q(1, lambda j: 1 + 4 * j, 4)
    each_q("near", 1, 1)
    slab_q(1, lambda j: 3 + 4 * j, 4)
    each_q("near", 1, 0)
    each_q("near", 2, 1)
    each_q("near", 2, 0)
    slab_q(0, lambda j: j, 4)
    slab_q(1, lambda j: 4 * j, 4)

    sets = {
        "q": (0, sum_q, held_q, new_q, x_q, Q_ROWS, Q_COLS),
        "k": (1, sum_k, held_k, new_k, x_k, KV_ROWS, KV_COLS),
    }

    def slot(kind, owner, c):
        _, _, _, _, x_ref, rows, cols = sets[kind]
        return x_ref.at[
            pl.ds(pl.multiple_of(lax.rem(owner, 2) * rows, rows), rows),
            pl.ds(pl.multiple_of(c * cols, cols), cols),
        ]

    def group_copy(kind, k, source, target):
        return pltpu.make_async_remote_copy(
            src_ref=source,
            dst_ref=target,
            send_sem=ag_send.at[sets[kind][0], k],
            recv_sem=ag_recv.at[sets[kind][0], k],
            device_id=group[k],
            device_id_type=MESH,
        )

    def gather(kind):
        index, total, held, new_ref, _, _, _ = sets[kind]
        load_held[1 - index].wait()
        gradient = total[...]
        renewed = momentum_rate * held[...] + gradient
        prepared = gradient + momentum_rate * renewed
        mine = slot(kind, me, core)
        mine[...] = prepared.astype(jnp.bfloat16)
        for k in (1, 0) if kind == "q" else (1, 2, 0):
            copy = group_copy(kind, k, mine, mine)
            copy.start()
            started.append(copy)
        new_ref[...] = renewed

    def forward(kind):
        theirs = slot(kind, *group[1])
        group_copy(kind, 1, slot(kind, me, core), theirs).wait_recv()
        copy = pltpu.make_async_remote_copy(
            src_ref=theirs,
            dst_ref=theirs,
            send_sem=ag_send.at[sets[kind][0], 2],
            recv_sem=ag_recv.at[sets[kind][0], 2],
            device_id=group[0],
            device_id_type=MESH,
        )
        copy.start()
        started.append(copy)

    def end(kind):
        for k in (0, 2) if kind == "q" else (0, 1, 2):
            group_copy(kind, k, slot(kind, me, core), slot(kind, *group[k])).wait_recv()

    for item in PLAN:
        act, name = item.split()
        if act == "products":
            load_lk.wait()
            lax.fori_loop(0, 16, unit_k, 0)
        elif act in ("far", "near"):
            for s in range(3):
                for half in range(2):
                    getattr(chunks[name], act)(s, half)
        elif act in ("relay1", "second", "relay2", "third"):
            for s in range(3):
                getattr(chunks[name], act)(s)
        elif act == "last":
            half = int(name[1])
            for s in range(3):
                total = chunks[name].total(s)
                if name[0] == "q":
                    lane = s * SLAB + half * LANES
                    sum_q[:, lane:lane + LANES] = total
                else:
                    at, rows = KV_CUT[s]
                    sum_k[at:at + rows, half * LANES:(half + 1) * LANES] = total
        elif act == "gather":
            gather(name)
        elif act == "forward":
            forward(name)
        elif act == "end":
            end(name)
    for copy in started:
        copy.wait_send()


def closing(
    prep_k, prep_q, new_k, new_q, out_uk, out_nk, out_uq, out_nq,
    x_k, x_q, mix_k, mix_q, up_k, up_q, sem,
):
    moves = ((new_k, out_nk), (new_q, out_nq), (up_k, out_uk), (up_q, out_uq))
    moves = [pltpu.make_async_copy(a, b, sem.at[k]) for k, (a, b) in enumerate(moves)]
    moves[0].start()
    moves[1].start()
    newton(((prep_k, x_k, mix_k, up_k), (prep_q, x_q, mix_q, up_q)))
    moves[2].start()
    moves[3].start()
    for move in moves:
        move.wait()


def per_device(latent_kv, latent_q, grad_kv, grad_q, momentum_kv, momentum_q):
    arrays = (latent_kv, latent_q, grad_kv, grad_q, momentum_kv, momentum_q)
    arrays = [pltpu.with_memory_space_constraint(array, pltpu.HBM) for array in arrays]
    low, full = jnp.bfloat16, jnp.float32
    cuts = (Q_CUT, Q_CUT, KV_CUT, KV_CUT)

    def cells(*lead):
        return [[pltpu.VMEM(lead + (rows, LANES), low) for _, rows in cut] for cut in cuts]

    vmem = pl.BlockSpec(memory_space=pltpu.VMEM)
    hbm = pl.BlockSpec(memory_space=pl.ANY)
    middle = pl.pallas_call(
        kernel,
        out_shape=(
            pltpu.VMEM((2 * KV_ROWS, 2 * KV_COLS), low),
            pltpu.VMEM((2 * Q_ROWS, 2 * Q_COLS), low),
            pltpu.VMEM((KV_ROWS, KV_COLS), full),
            pltpu.VMEM((Q_ROWS, Q_COLS), full),
        ),
        in_specs=[hbm] * 6,
        out_specs=(vmem,) * 4,
        scratch_shapes=[
            pltpu.VMEM((TOK, KV_COLS), low),
            pltpu.VMEM((TOK, Q_COLS), low),
            pltpu.VMEM((16, TOK, 4 * KV_ROWS), low),
            pltpu.VMEM((16, TOK, 4 * Q_ROWS), low),
            cells(4, 4, 4),
            cells(6, 2, 4),
            cells(12),
            cells(3),
            pltpu.VMEM((KV_ROWS, KV_COLS), full),
            pltpu.VMEM((Q_ROWS, Q_COLS), full),
            pltpu.VMEM((KV_ROWS, KV_COLS), full),
            pltpu.VMEM((Q_ROWS, Q_COLS), full),
            pltpu.SemaphoreType.DMA((6,)),
            pltpu.SemaphoreType.DMA((16,)),
            pltpu.SemaphoreType.DMA((16,)),
            pltpu.SemaphoreType.DMA((4, 3, SLOTS)),
            pltpu.SemaphoreType.DMA((4, 3, SLOTS)),
            pltpu.SemaphoreType.DMA((2, 3)),
            pltpu.SemaphoreType.DMA((2, 3)),
        ],
        compiler_params=pltpu.CompilerParams(
            collective_id=0, has_side_effects=True, vmem_limit_bytes=50 * 2**20
        ),
        name="sum_all",
    )(*arrays)
    return pl.pallas_call(
        closing,
        out_shape=(
            jax.ShapeDtypeStruct((KV_ROWS, KV_COLS), low),
            jax.ShapeDtypeStruct((KV_ROWS, KV_COLS), full),
            jax.ShapeDtypeStruct((Q_ROWS, Q_COLS), low),
            jax.ShapeDtypeStruct((Q_ROWS, Q_COLS), full),
        ),
        in_specs=[vmem] * 4,
        out_specs=(hbm,) * 4,
        scratch_shapes=[
            pltpu.VMEM((2 * KV_ROWS, 2 * KV_COLS), low),
            pltpu.VMEM((2 * Q_ROWS, 2 * Q_COLS), low),
            pltpu.VMEM((2 * KV_ROWS, 2 * KV_ROWS), low),
            pltpu.VMEM((2 * Q_ROWS, 2 * Q_ROWS), low),
            pltpu.VMEM((KV_ROWS, KV_COLS), low),
            pltpu.VMEM((Q_ROWS, Q_COLS), low),
            pltpu.SemaphoreType.DMA((4,)),
        ],
        compiler_params=pltpu.CompilerParams(vmem_limit_bytes=24 * 2**20),
        name="closing",
    )(*middle)


def solution(mesh):
    in_specs = (
        P("dp", "tensor"),
        P("dp", "tensor"),
        P("dp", None),
        P("dp", None),
        P("dp", "tensor"),
        P("dp", "tensor"),
    )
    out_specs = (P("dp", "tensor"), P("dp", "tensor"), P("dp", "tensor"), P("dp", "tensor"))
    return jax.shard_map(
        per_device, mesh=mesh, in_specs=in_specs, out_specs=out_specs, check_vma=False
    )
```

```python
import functools

import jax
import jax.numpy as jnp
from jax import lax
from jax.experimental import pallas as pl
from jax.experimental.pallas import tpu as pltpu
from jax.sharding import PartitionSpec as P

ITERS = 5
SIDE = 4
MESH = pl.DeviceIdType.MESH

first_coef = 3.4445
second_coef = -4.775
third_coef = 2.0315
momentum_rate = 0.95
norm_eps = 1e-07

TOK = 512
KV_ROWS, KV_COLS = 128, 256
Q_ROWS, Q_COLS = 96, 768
LANES = 128
SLAB = 2 * LANES
ORDERS = ("xzy", "zyx", "yxz")
KV_CUT = ((0, 48), (48, 48), (96, 32))
Q_CUT = ((0, 96),) * 3
SECOND, THIRD, FOURTH = 6, 12, 15
SLOTS = 17
FORWARDED = ("q0", "q1", "k0")
RINGS = ("q0", "q1", "k0")

PLAN = (
    "near q1", "relay1 q1", "relay1 q0", "products k", "far k0", "near k0", "second q1",
    "second q0", "relay1 k0", "far k1", "relay2 q0", "relay2 q1", "second k0", "near k1",
    "relay1 k1", "third q1", "third q0", "relay2 k0", "second k1", "last q0", "gather q0",
    "third k0", "third k1", "last q1", "gather q1", "last k0", "gather k0", "last k1",
    "gather k1", "forward q1", "forward q0", "end q0", "forward k0", "end k0", "end k1",
    "end q1",
)


def shifted(where, axis, step):
    moved = dict(where)
    moved[axis] = lax.rem(moved[axis] + step + SIDE, SIDE)
    return (moved["x"] * SIDE + moved["z"]) * SIDE + moved["y"]


def gram_of(matrix):
    return lax.dot_general(
        matrix, matrix, (((1,), (1,)), ((), ())), preferred_element_type=jnp.float32
    )


def mixers(grams):
    lows = [gram.astype(jnp.bfloat16) for gram in grams]
    squares = [jnp.dot(low, low, preferred_element_type=jnp.float32) for low in lows]
    return [
        (second_coef * low.astype(jnp.float32) + third_coef * square).astype(jnp.bfloat16)
        for low, square in zip(lows, squares)
    ]


def advance(iterate, mixing, source, scale=None):
    moved = jnp.dot(mixing, source, preferred_element_type=jnp.float32)
    total = first_coef * iterate.astype(jnp.float32) + moved
    if scale is not None:
        total = total * scale
    return total.astype(jnp.bfloat16)


def scale_of(gram):
    at = [lax.broadcasted_iota(jnp.int32, gram.shape, d) for d in range(2)]
    squares = jnp.sum(jnp.where(at[0] == at[1], gram, 0.0), keepdims=True)
    return 1.0 / (jnp.sqrt(squares) + norm_eps)


def newton(heads):
    own_row, own_col = lax.rem(lax.axis_index("dp"), 2), lax.axis_index("tensor")
    for sweep in range(ITERS):
        source = [head[0] if sweep == 0 else head[1] for head in heads]
        wholes = [ref[...] for ref in source]
        grams = [gram_of(whole) for whole in wholes]
        scales = [None] * len(heads)
        if sweep == 0:
            scales = [scale_of(gram) for gram in grams]
            grams = [gram * scale * scale for gram, scale in zip(grams, scales)]
        mixings = mixers(grams)
        for head, whole, mixing, scale in zip(heads, wholes, mixings, scales):
            _, x_ref, mix_ref, out_ref = head
            if sweep < ITERS - 1:
                x_ref[...] = advance(whole, mixing, whole, scale)
                continue
            mix_ref[...] = mixing
            rows, cols = out_ref.shape
            own_rows = pl.ds(pl.multiple_of(own_row * rows, rows), rows)
            own_cols = pl.ds(pl.multiple_of(own_col * cols, cols), cols)
            own = advance(
                x_ref[own_rows, own_cols], mix_ref[own_rows, :], x_ref[:, own_cols]
            )
            slabs = cols // (2 * LANES)
            for at in range(2 * slabs):
                lane = (at % slabs * 2 + at // slabs) * LANES
                out_ref[:, lane:lane + LANES] = own[:, at * LANES:(at + 1) * LANES]


def add_into(target, others, count):
    def step(i, carry):
        total = target[i].astype(jnp.float32)
        for other in others:
            total += other[i].astype(jnp.float32)
        target[i] = total.astype(target.dtype)
        return carry

    lax.fori_loop(0, count, step, 0)


def kernel(
    lat_kv, lat_q, grad_kv, grad_q, mom_kv, mom_q,
    x_k, x_q, new_k, new_q,
    lk, lq, gk, gq, parts, ones, twos, threes, sum_k, sum_q, held_k, held_q,
    in_sem, gk_sem, gq_sem, send_sem, recv_sem, ag_send, ag_recv,
):
    me = lax.axis_index("dp")
    core = lax.axis_index("tensor")
    where = {"x": me // 16, "z": lax.rem(me // 4, 4), "y": lax.rem(me, 4)}
    low = lax.rem(me, 2)
    twin = me + 1 - 2 * low
    group = ((me, 1 - core), (twin, core), (twin, 1 - core))

    barrier = pltpu.get_barrier_semaphore()
    friends = [(shifted(where, a, s), core) for a in "xyz" for s in (1, 2, 3)]
    friends += [group[0], group[2]]
    for friend in friends:
        pl.semaphore_signal(barrier, inc=1, device_id=friend, device_id_type=MESH)

    def fetch(source, target, sems, width, i):
        u = lax.rem(where["x"] + i // 4, 4) * 4 + lax.rem(where["z"] + lax.rem(i, 4), 4)
        at = pl.multiple_of(u * width, 128)
        return pltpu.make_async_copy(source.at[:, pl.ds(at, width)], target.at[i], sems.at[i])

    fetch_q = functools.partial(fetch, grad_q, gq, gq_sem, 4 * Q_ROWS)
    fetch_k = functools.partial(fetch, grad_kv, gk, gk_sem, 4 * KV_ROWS)
    load_lq = [
        pltpu.make_async_copy(
            lat_q.at[:, pl.ds(k * SLAB, SLAB)], lq.at[:, pl.ds(k * SLAB, SLAB)], in_sem.at[k]
        )
        for k in range(3)
    ]
    load_lk = pltpu.make_async_copy(lat_kv, lk, in_sem.at[3])
    load_held = [
        pltpu.make_async_copy(mom_kv, held_k, in_sem.at[4]),
        pltpu.make_async_copy(mom_q, held_q, in_sem.at[5]),
    ]
    load_lq[0].start()
    for i in (8, 9, 10, 11):
        fetch_q(i).start()
    load_lq[2].start()
    for i in (0, 1, 2, 3):
        fetch_q(i).start()
    load_lq[1].start()
    for i in (6, 14, 12, 13, 15, 4, 5, 7):
        fetch_q(i).start()

    started = []

    class Chunk:
        def __init__(self, index, ring):
            self.index, self.ring = index, ring
            self.parts, self.ones = parts[index], ones[index]
            self.twos, self.threes = twos[index], threes[index]
            self.copies, self.split = {}, set()

        def go(self, s, slot, source, target, axis, step):
            copy = pltpu.make_async_remote_copy(
                src_ref=source,
                dst_ref=target,
                send_sem=send_sem.at[self.index, s, slot],
                recv_sem=recv_sem.at[self.index, s, slot],
                device_id=(shifted(where, axis, step), core),
                device_id_type=MESH,
            )
            copy.start()
            started.append(copy)
            self.copies[s, slot] = copy

        def arrived(self, s, *slots):
            for slot in slots:
                self.copies[s, slot].wait_recv()

        def far(self, s, half):
            part, got, axis = self.parts[s], self.ones[s], ORDERS[s][0]
            step = 1 if half == 0 else -1
            self.go(s, half, part.at[2, pl.ds(2 * half, 2)], got.at[half], axis, step)

        def far_one(self, s, b):
            part, got, axis = self.parts[s], self.ones[s], ORDERS[s][0]
            half, at = b // 2, b % 2
            slot = FOURTH + half if at else half
            step = 1 if half == 0 else -1
            self.go(s, slot, part.at[2, b], got.at[half, at], axis, step)
            self.split.add(s)

        def far_in(self, s, half):
            self.arrived(s, half)
            if s in self.split:
                self.arrived(s, FOURTH + half)

        def near(self, s, half):
            part, got, axis = self.parts[s], self.ones[s], ORDERS[s][0]
            if half == 0:
                self.go(s, 3, part.at[3, pl.ds(0, 2)], got.at[3], axis, -1)
            else:
                self.go(s, 2, part.at[1, pl.ds(2, 2)], got.at[2], axis, 1)

        def relay1(self, s):
            part, got, axis = self.parts[s], self.ones[s], ORDERS[s][0]
            self.far_in(s, 0)
            for b in range(2):
                add_into(part.at[1, b], [got.at[0, b]], 4)
            self.go(s, 4, part.at[1, pl.ds(0, 2)], got.at[4], axis, 1)
            self.far_in(s, 1)
            for b in range(2):
                add_into(part.at[3, 2 + b], [got.at[1, b]], 4)
            self.go(s, 5, part.at[3, pl.ds(2, 2)], got.at[5], axis, -1)

        def second(self, s):
            part, got, two, axis = self.parts[s], self.ones[s], self.twos[s], ORDERS[s][1]
            self.arrived(s, 2, 5)
            add_into(part.at[0, 2], [got.at[2, 0], got.at[5, 0]], 4)
            if self.ring:
                for half, step in ((0, 1), (1, -1)):
                    self.go(
                        s, SECOND + half, part.at[0, 2, pl.ds(2 * half, 2)],
                        two.at[pl.ds(2 * half, 2)], axis, step,
                    )
            else:
                self.go(s, SECOND + 1, part.at[0, 2], two.at[pl.ds(4, 4)], axis, 2)
            add_into(part.at[0, 3], [got.at[2, 1], got.at[5, 1]], 4)
            if self.ring:
                self.go(s, SECOND + 3, part.at[0, 3, pl.ds(0, 2)], two.at[pl.ds(6, 2)], axis, -1)
            else:
                self.go(s, SECOND + 2, part.at[0, 3], two.at[pl.ds(8, 4)], axis, 3)
            self.arrived(s, 3, 4)
            add_into(part.at[0, 1], [got.at[3, 1], got.at[4, 1]], 4)
            if self.ring:
                self.go(s, SECOND + 2, part.at[0, 1, pl.ds(2, 2)], two.at[pl.ds(4, 2)], axis, 1)
            else:
                self.go(s, SECOND, part.at[0, 1], two.at[pl.ds(0, 4)], axis, 1)
            add_into(part.at[0, 0], [got.at[3, 0], got.at[4, 0]], 4)

        def relay2(self, s):
            part, two, axis = self.parts[s], self.twos[s], ORDERS[s][1]
            for half, b, step in ((0, 1, 1), (1, 3, -1)):
                held = part.at[0, b, pl.ds(2 * half, 2)]
                self.arrived(s, SECOND + half)
                add_into(held, [two.at[pl.ds(2 * half, 2)]], 2)
                self.go(
                    s, SECOND + 4 + half, held, two.at[pl.ds(8 + 2 * half, 2)], axis, step
                )

        def third(self, s):
            part, two, three, axis = self.parts[s], self.twos[s], self.threes[s], ORDERS[s][2]
            if self.ring:
                for half, slots in ((0, (3, 4)), (1, (2, 5))):
                    self.arrived(s, *(SECOND + k for k in slots))
                    add_into(
                        part.at[0, 0, pl.ds(2 * half, 2)],
                        [two.at[pl.ds(2 * k, 2)] for k in slots], 2,
                    )
            else:
                self.arrived(s, *(SECOND + k for k in range(3)))
                add_into(part.at[0, 0], [two.at[pl.ds(4 * k, 4)] for k in range(3)], 4)
            for c in (2, 1, 3):
                self.go(s, THIRD - 1 + c, part.at[0, 0, c], three.at[c - 1], axis, c)

        def total(self, s):
            part, three = self.parts[s], self.threes[s]
            self.arrived(s, *(THIRD + k for k in range(3)))
            total = part[0, 0, 0].astype(jnp.float32)
            for c in range(3):
                total += three[c].astype(jnp.float32)
            return total

    chunks = {name: Chunk(at, name in RINGS) for at, name in enumerate(("q0", "q1", "k0", "k1"))}

    def store(pair, cuts, stride, s, i, term, lanes_from):
        xr, zr = i // 4, i % 4
        at, rows = cuts[s]
        for y in range(4):
            place = {"x": xr, "z": zr, "y": lax.rem(y - where["y"] + 4, 4)}
            place = tuple(place[a] for a in ORDERS[s])
            for half in range(2):
                lane = lanes_from + half * LANES
                chunks[pair[half]].parts[s][place] = term[
                    y * stride + at:y * stride + at + rows, lane:lane + LANES
                ]

    def slab_q(s, unit_of, count):
        for i in (unit_of(j) for j in range(count)):
            term = lax.dot_general(
                gq[i], lq[:, s * SLAB:(s + 1) * SLAB], (((0,), (0,)), ((), ())),
                preferred_element_type=jnp.float32,
            ).astype(jnp.bfloat16)
            store(("q0", "q1"), Q_CUT, Q_ROWS, s, i, term, 0)

    def unit_k(i):
        term = lax.dot_general(
            gk[i], lk[...], (((0,), (0,)), ((), ())), preferred_element_type=jnp.float32
        ).astype(jnp.bfloat16)
        for s in range(3):
            store(("k0", "k1"), KV_CUT, KV_ROWS, s, i, term, 0)

    def units_k(j, carry):
        for i in range(4):
            fetch_k(4 * j + i).wait()
        for i in range(4):
            unit_k(4 * j + i)
        return carry

    q_ready = []

    def need_q(*units):
        for i in units:
            if i not in q_ready:
                q_ready.append(i)
                fetch_q(i).wait()

    def each_q(act, *args):
        for name in ("q0", "q1"):
            getattr(chunks[name], act)(*args)

    big, small = chunks["q0"], chunks["q1"]
    load_lq[0].wait()
    need_q(8, 9)
    slab_q(0, lambda j: 8 + j, 2)
    pl.semaphore_wait(barrier, len(friends))
    big.far(0, 0)
    need_q(10, 11)
    slab_q(0, lambda j: 10 + j, 2)
    big.far(0, 1)
    load_lq[2].wait()
    slab_q(2, lambda j: 8 + j, 4)
    each_q("far_one", 2, 2)
    need_q(0, 1, 2, 3)
    slab_q(2, lambda j: j, 4)
    each_q("far_one", 2, 0)
    load_lq[1].wait()
    need_q(6, 14)
    slab_q(1, lambda j: 2 + 4 * j, 4)
    big.far(1, 0)
    big.far(1, 1)
    load_lk.start()
    for i in range(16):
        fetch_k(i).start()
    for load in load_held:
        load.start()
    need_q(4, 5, 7, 12, 13, 15)
    slab_q(0, lambda j: 6 + j, 2)
    big.near(0, 1)
    slab_q(0, lambda j: 12 + j, 2)
    big.near(0, 0)
    small.far(0, 0)
    small.far(0, 1)
    slab_q(2, lambda j: 12 + j, 4)
    big.far_one(2, 3)
    big.near(2, 1)
    slab_q(2, lambda j: 4 + j, 4)
    big.far_one(2, 1)
    big.near(2, 0)
    small.far_one(2, 3)
    small.far_one(2, 1)
    slab_q(1, lambda j: 1 + 4 * j, 4)
    big.near(1, 1)
    slab_q(1, lambda j: 3 + 4 * j, 4)
    big.near(1, 0)
    small.far(1, 0)
    small.far(1, 1)
    slab_q(0, lambda j: 4 + j, 2)
    slab_q(0, lambda j: 14 + j, 2)
    slab_q(0, lambda j: j, 4)
    slab_q(1, lambda j: 4 * j, 4)

    kinds = {
        "q": (sum_q, held_q, new_q, x_q, Q_ROWS, 3 * LANES),
        "k": (sum_k, held_k, new_k, x_k, KV_ROWS, LANES),
    }

    def slot(name, owner, c):
        _, _, _, x_ref, rows, cols = kinds[name[0]]
        return x_ref.at[
            pl.ds(pl.multiple_of(lax.rem(owner, 2) * rows, rows), rows),
            pl.ds(pl.multiple_of((c * 2 + int(name[1])) * cols, LANES), cols),
        ]

    def group_copy(name, k, source, target, way=None):
        index = chunks[name].index
        return pltpu.make_async_remote_copy(
            src_ref=source,
            dst_ref=target,
            send_sem=ag_send.at[index, k],
            recv_sem=ag_recv.at[index, k],
            device_id=group[k if way is None else way],
            device_id_type=MESH,
        )

    def gather(name):
        total, held, new_ref, x_ref, rows, cols = kinds[name[0]]
        if name in ("q0", "k0"):
            load_held["kq".index(name[0])].wait()
        for t in range(cols // LANES):
            at = pl.ds((2 * t + int(name[1])) * LANES, LANES)
            gradient = total[:, at]
            renewed = momentum_rate * held[:, at] + gradient
            prepared = gradient + momentum_rate * renewed
            new_ref[:, at] = renewed
            part = pl.ds(
                pl.multiple_of((core * 2 + int(name[1])) * cols + t * LANES, LANES), LANES
            )
            x_ref[pl.ds(pl.multiple_of(low * rows, rows), rows), part] = prepared.astype(
                jnp.bfloat16
            )
        mine = slot(name, me, core)
        for k in (1, 0) if name in FORWARDED else (1, 2, 0):
            copy = group_copy(name, k, mine, mine)
            copy.start()
            started.append(copy)

    def forward(name):
        theirs = slot(name, *group[1])
        group_copy(name, 1, slot(name, me, core), theirs).wait_recv()
        copy = group_copy(name, 2, theirs, theirs, 0)
        copy.start()
        started.append(copy)

    def end(name):
        for k in (0, 2) if name in FORWARDED else (0, 1, 2):
            group_copy(name, k, slot(name, me, core), slot(name, *group[k])).wait_recv()

    for item in PLAN:
        act, name = item.split()
        if act == "products":
            load_lk.wait()
            lax.fori_loop(0, 4, units_k, 0)
        elif act in ("far", "near"):
            for s in range(3):
                for half in range(2):
                    getattr(chunks[name], act)(s, half)
        elif act in ("relay1", "second", "relay2", "third"):
            for s in range(3):
                getattr(chunks[name], act)(s)
        elif act == "last":
            half = int(name[1])
            for s in range(3):
                total = chunks[name].total(s)
                if name[0] == "q":
                    lane = s * SLAB + half * LANES
                    sum_q[:, lane:lane + LANES] = total
                else:
                    at, rows = KV_CUT[s]
                    sum_k[at:at + rows, half * LANES:(half + 1) * LANES] = total
        elif act == "gather":
            gather(name)
        elif act == "forward":
            forward(name)
        elif act == "end":
            end(name)
    for copy in started:
        copy.wait_send()


def closing(
    prep_k, prep_q, new_k, new_q, out_uk, out_nk, out_uq, out_nq,
    x_k, x_q, mix_k, mix_q, up_k, up_q, sem,
):
    moves = ((new_k, out_nk), (new_q, out_nq), (up_k, out_uk), (up_q, out_uq))
    moves = [pltpu.make_async_copy(a, b, sem.at[k]) for k, (a, b) in enumerate(moves)]
    moves[0].start()
    moves[1].start()
    newton(((prep_k, x_k, mix_k, up_k), (prep_q, x_q, mix_q, up_q)))
    moves[2].start()
    moves[3].start()
    for move in moves:
        move.wait()


def per_device(latent_kv, latent_q, grad_kv, grad_q, momentum_kv, momentum_q):
    arrays = (latent_kv, latent_q, grad_kv, grad_q, momentum_kv, momentum_q)
    arrays = [pltpu.with_memory_space_constraint(array, pltpu.HBM) for array in arrays]
    low, full = jnp.bfloat16, jnp.float32
    cuts = (Q_CUT, Q_CUT, KV_CUT, KV_CUT)

    def cells(*lead):
        return [[pltpu.VMEM(lead + (rows, LANES), low) for _, rows in cut] for cut in cuts]

    vmem = pl.BlockSpec(memory_space=pltpu.VMEM)
    hbm = pl.BlockSpec(memory_space=pl.ANY)
    middle = pl.pallas_call(
        kernel,
        out_shape=(
            pltpu.VMEM((2 * KV_ROWS, 2 * KV_COLS), low),
            pltpu.VMEM((2 * Q_ROWS, 2 * Q_COLS), low),
            pltpu.VMEM((KV_ROWS, KV_COLS), full),
            pltpu.VMEM((Q_ROWS, Q_COLS), full),
        ),
        in_specs=[hbm] * 6,
        out_specs=(vmem,) * 4,
        scratch_shapes=[
            pltpu.VMEM((TOK, KV_COLS), low),
            pltpu.VMEM((TOK, Q_COLS), low),
            pltpu.VMEM((16, TOK, 4 * KV_ROWS), low),
            pltpu.VMEM((16, TOK, 4 * Q_ROWS), low),
            cells(4, 4, 4),
            cells(6, 2, 4),
            cells(12),
            cells(3),
            pltpu.VMEM((KV_ROWS, KV_COLS), full),
            pltpu.VMEM((Q_ROWS, Q_COLS), full),
            pltpu.VMEM((KV_ROWS, KV_COLS), full),
            pltpu.VMEM((Q_ROWS, Q_COLS), full),
            pltpu.SemaphoreType.DMA((6,)),
            pltpu.SemaphoreType.DMA((16,)),
            pltpu.SemaphoreType.DMA((16,)),
            pltpu.SemaphoreType.DMA((4, 3, SLOTS)),
            pltpu.SemaphoreType.DMA((4, 3, SLOTS)),
            pltpu.SemaphoreType.DMA((4, 3)),
            pltpu.SemaphoreType.DMA((4, 3)),
        ],
        compiler_params=pltpu.CompilerParams(
            collective_id=0, has_side_effects=True, vmem_limit_bytes=50 * 2**20
        ),
        name="sum_all",
    )(*arrays)
    return pl.pallas_call(
        closing,
        out_shape=(
            jax.ShapeDtypeStruct((KV_ROWS, KV_COLS), low),
            jax.ShapeDtypeStruct((KV_ROWS, KV_COLS), full),
            jax.ShapeDtypeStruct((Q_ROWS, Q_COLS), low),
            jax.ShapeDtypeStruct((Q_ROWS, Q_COLS), full),
        ),
        in_specs=[vmem] * 4,
        out_specs=(hbm,) * 4,
        scratch_shapes=[
            pltpu.VMEM((2 * KV_ROWS, 2 * KV_COLS), low),
            pltpu.VMEM((2 * Q_ROWS, 2 * Q_COLS), low),
            pltpu.VMEM((2 * KV_ROWS, 2 * KV_ROWS), low),
            pltpu.VMEM((2 * Q_ROWS, 2 * Q_ROWS), low),
            pltpu.VMEM((KV_ROWS, KV_COLS), low),
            pltpu.VMEM((Q_ROWS, Q_COLS), low),
            pltpu.SemaphoreType.DMA((4,)),
        ],
        compiler_params=pltpu.CompilerParams(vmem_limit_bytes=24 * 2**20),
        name="closing",
    )(*middle)


def solution(mesh):
    in_specs = (
        P("dp", "tensor"),
        P("dp", "tensor"),
        P("dp", None),
        P("dp", None),
        P("dp", "tensor"),
        P("dp", "tensor"),
    )
    out_specs = (P("dp", "tensor"), P("dp", "tensor"), P("dp", "tensor"), P("dp", "tensor"))
    return jax.shard_map(
        per_device, mesh=mesh, in_specs=in_specs, out_specs=out_specs, check_vma=False
    )
```

```python
import functools

import jax
import jax.numpy as jnp
from jax import lax
from jax.experimental import pallas as pl
from jax.experimental.pallas import tpu as pltpu
from jax.sharding import PartitionSpec as P

ITERS = 5
SIDE = 4
MESH = pl.DeviceIdType.MESH

first_coef = 3.4445
second_coef = -4.775
third_coef = 2.0315
momentum_rate = 0.95
norm_eps = 1e-07

TOK = 512
KV_ROWS, KV_COLS = 128, 256
Q_ROWS, Q_COLS = 96, 768
LANES = 128
SLAB = 2 * LANES
ORDERS = ("xzy", "zyx", "yxz")
KV_CUT = ((0, 48), (48, 48), (96, 32))
Q_CUT = ((0, 96),) * 3
FORWARDED = ("q0", "q1", "k0")
RINGS = ("q0", "q1", "k0")

PLAN = (
    "near q1", "relay1 q1", "relay1 q0", "products k", "far k0", "near k0", "second q1",
    "second q0", "relay1 k0", "far k1", "relay2 q0", "relay2 q1", "second k0", "near k1",
    "relay1 k1", "third q1", "third q0", "relay2 k0", "second k1", "last q0", "gather q0",
    "third k0", "third k1", "last q1", "gather q1", "last k0", "gather k0", "last k1",
    "gather k1", "forward q1", "forward q0", "end q0", "forward k0", "end k0", "end k1",
    "end q1",
)


def shifted(where, axis, step):
    moved = dict(where)
    moved[axis] = lax.rem(moved[axis] + step + SIDE, SIDE)
    return (moved["x"] * SIDE + moved["z"]) * SIDE + moved["y"]


def gram_of(matrix):
    return lax.dot_general(
        matrix, matrix, (((1,), (1,)), ((), ())), preferred_element_type=jnp.float32
    )


def mixers(grams):
    lows = [gram.astype(jnp.bfloat16) for gram in grams]
    squares = [jnp.dot(low, low, preferred_element_type=jnp.float32) for low in lows]
    return [
        (second_coef * low.astype(jnp.float32) + third_coef * square).astype(jnp.bfloat16)
        for low, square in zip(lows, squares)
    ]


def advance(iterate, mixing, source, scale=None):
    moved = jnp.dot(mixing, source, preferred_element_type=jnp.float32)
    total = first_coef * iterate.astype(jnp.float32) + moved
    if scale is not None:
        total = total * scale
    return total.astype(jnp.bfloat16)


def scale_of(gram):
    at = [lax.broadcasted_iota(jnp.int32, gram.shape, d) for d in range(2)]
    squares = jnp.sum(jnp.where(at[0] == at[1], gram, 0.0), keepdims=True)
    return 1.0 / (jnp.sqrt(squares) + norm_eps)


def newton(heads):
    own_row, own_col = lax.rem(lax.axis_index("dp"), 2), lax.axis_index("tensor")
    for sweep in range(ITERS):
        source = [head[0] if sweep == 0 else head[1] for head in heads]
        wholes = [ref[...] for ref in source]
        grams = [gram_of(whole) for whole in wholes]
        scales = [None] * len(heads)
        if sweep == 0:
            scales = [scale_of(gram) for gram in grams]
            grams = [gram * scale * scale for gram, scale in zip(grams, scales)]
        mixings = mixers(grams)
        for head, whole, mixing, scale in zip(heads, wholes, mixings, scales):
            _, x_ref, mix_ref, out_ref = head
            if sweep < ITERS - 1:
                x_ref[...] = advance(whole, mixing, whole, scale)
                continue
            mix_ref[...] = mixing
            rows, cols = out_ref.shape
            own_rows = pl.ds(pl.multiple_of(own_row * rows, rows), rows)
            own_cols = pl.ds(pl.multiple_of(own_col * cols, cols), cols)
            own = advance(
                x_ref[own_rows, own_cols], mix_ref[own_rows, :], x_ref[:, own_cols]
            )
            slabs = cols // (2 * LANES)
            for at in range(2 * slabs):
                lane = (at % slabs * 2 + at // slabs) * LANES
                out_ref[:, lane:lane + LANES] = own[:, at * LANES:(at + 1) * LANES]


def add_into(target, others, count):
    def step(i, carry):
        total = target[i].astype(jnp.float32)
        for other in others:
            total += other[i].astype(jnp.float32)
        target[i] = total.astype(target.dtype)
        return carry

    lax.fori_loop(0, count, step, 0)


def kernel(
    lat_kv, lat_q, grad_kv, grad_q, mom_kv, mom_q,
    x_k, x_q, new_k, new_q,
    lk, lq, gk, gq, parts, ones, twos, threes, sum_k, sum_q, held_k, held_q,
    in_sem, gk_sem, gq_sem, send_sem, recv_sem, ag_send, ag_recv,
):
    me = lax.axis_index("dp")
    core = lax.axis_index("tensor")
    where = {"x": me // 16, "z": lax.rem(me // 4, 4), "y": lax.rem(me, 4)}
    low = lax.rem(me, 2)
    twin = me + 1 - 2 * low
    group = ((me, 1 - core), (twin, core), (twin, 1 - core))

    barrier = pltpu.get_barrier_semaphore()
    friends = [(shifted(where, a, s), core) for a in "xyz" for s in (1, 2, 3)]
    friends += [group[0], group[2]]
    for friend in friends:
        pl.semaphore_signal(barrier, inc=1, device_id=friend, device_id_type=MESH)

    def fetch(source, target, sem, width, i):
        u = lax.rem(where["x"] + i // 4, 4) * 4 + lax.rem(where["z"] + lax.rem(i, 4), 4)
        at = pl.multiple_of(u * width, 128)
        return pltpu.make_async_copy(source.at[:, pl.ds(at, width)], target.at[i], sem)

    q_sets = ((8, 9), (10, 11), (0, 1, 2, 3), (6, 14), (4, 5, 7, 12, 13, 15))

    def start_q(k):
        for i in q_sets[k]:
            fetch(grad_q, gq, gq_sem.at[k], 4 * Q_ROWS, i).start()

    def need_q(k):
        many = gq.at[pl.ds(0, len(q_sets[k]))]
        pltpu.make_async_copy(many, many, gq_sem.at[k]).wait()

    def start_k():
        for i in range(16):
            fetch(grad_kv, gk, gk_sem.at[i // 4], 4 * KV_ROWS, i).start()

    load_lq = [
        pltpu.make_async_copy(
            lat_q.at[:, pl.ds(k * SLAB, SLAB)], lq.at[:, pl.ds(k * SLAB, SLAB)], in_sem.at[k]
        )
        for k in range(3)
    ]
    load_lk = pltpu.make_async_copy(lat_kv, lk, in_sem.at[3])
    load_held = [
        pltpu.make_async_copy(mom_kv, held_k, in_sem.at[4]),
        pltpu.make_async_copy(mom_q, held_q, in_sem.at[5]),
    ]
    load_lq[0].start()
    start_q(0)
    start_q(1)
    load_lq[2].start()
    start_q(2)
    load_lq[1].start()
    start_q(3)
    start_q(4)

    def take(ref, sem):
        pltpu.make_async_remote_copy(
            src_ref=ref, dst_ref=ref, send_sem=sem, recv_sem=sem,
            device_id=group[0], device_id_type=MESH,
        ).wait_recv()

    def run(ref, start, count):
        return ref.at[pl.ds(start, count)]

    class Chunk:
        def __init__(self, index, ring):
            self.index, self.ring = index, ring
            self.parts, self.ones = parts[index], ones[index]
            self.twos, self.threes = twos[index], threes[index]

        def sem(self, s, stage):
            return recv_sem.at[self.index, 4 * s + stage]

        def go(self, s, stage, source, target, axis, step):
            pltpu.make_async_remote_copy(
                src_ref=source,
                dst_ref=target,
                send_sem=send_sem.at[self.index, s],
                recv_sem=self.sem(s, stage) if stage < 4 else recv_sem.at[self.index, 12],
                device_id=(shifted(where, axis, step), core),
                device_id_type=MESH,
            ).start()

        def sent(self):
            for s in range(3):
                take(run(self.parts[s], 0, 63), send_sem.at[self.index, s])

        def far(self, s, half):
            part, got, axis = self.parts[s], self.ones[s], ORDERS[s][0]
            step = 1 if half == 0 else -1
            self.go(s, 0, run(part, 32 + 8 * half, 8), run(got, 8 * half, 8), axis, step)

        def far_one(self, s, b):
            part, got, axis = self.parts[s], self.ones[s], ORDERS[s][0]
            step = 1 if b < 2 else -1
            self.go(s, 0, run(part, 32 + 4 * b, 4), run(got, 4 * b, 4), axis, step)

        def near(self, s, half):
            part, got, axis = self.parts[s], self.ones[s], ORDERS[s][0]
            if half == 0:
                self.go(s, 1, run(part, 48, 8), run(got, 24, 8), axis, -1)
            else:
                self.go(s, 1, run(part, 24, 8), run(got, 16, 8), axis, 1)

        def relay1(self, s):
            part, got, axis = self.parts[s], self.ones[s], ORDERS[s][0]
            take(run(got, 0, 16), self.sem(s, 0))
            add_into(run(part, 16, 8), [run(got, 0, 8)], 8)
            self.go(s, 1, run(part, 16, 8), run(got, 32, 8), axis, 1)
            add_into(run(part, 56, 8), [run(got, 8, 8)], 8)
            self.go(s, 1, run(part, 56, 8), run(got, 40, 8), axis, -1)

        def second(self, s):
            part, got, two, axis = self.parts[s], self.ones[s], self.twos[s], ORDERS[s][1]
            take(run(got, 16, 32), self.sem(s, 1))
            add_into(run(part, 8, 4), [run(got, 16, 4), run(got, 40, 4)], 4)
            if self.ring:
                self.go(s, 2, run(part, 8, 2), run(two, 0, 2), axis, 1)
                self.go(s, 2, run(part, 10, 2), run(two, 2, 2), axis, -1)
            else:
                self.go(s, 2, run(part, 8, 4), run(two, 4, 4), axis, 2)
            add_into(run(part, 12, 4), [run(got, 20, 4), run(got, 44, 4)], 4)
            if self.ring:
                self.go(s, 3, run(part, 12, 2), run(two, 6, 2), axis, -1)
            else:
                self.go(s, 2, run(part, 12, 4), run(two, 8, 4), axis, 3)
            add_into(run(part, 4, 4), [run(got, 28, 4), run(got, 36, 4)], 4)
            if self.ring:
                self.go(s, 3, run(part, 6, 2), run(two, 4, 2), axis, 1)
            else:
                self.go(s, 2, run(part, 4, 4), run(two, 0, 4), axis, 1)
            add_into(run(part, 0, 4), [run(got, 24, 4), run(got, 32, 4)], 4)

        def relay2(self, s):
            part, two, axis = self.parts[s], self.twos[s], ORDERS[s][1]
            take(run(two, 0, 4), self.sem(s, 2))
            add_into(run(part, 4, 2), [run(two, 0, 2)], 2)
            self.go(s, 3, run(part, 4, 2), run(two, 8, 2), axis, 1)
            add_into(run(part, 14, 2), [run(two, 2, 2)], 2)
            self.go(s, 3, run(part, 14, 2), run(two, 10, 2), axis, -1)

        def third(self, s):
            part, two, three, axis = self.parts[s], self.twos[s], self.threes[s], ORDERS[s][2]
            if self.ring:
                take(run(two, 4, 8), self.sem(s, 3))
                add_into(run(part, 0, 2), [run(two, 6, 2), run(two, 8, 2)], 2)
                add_into(run(part, 2, 2), [run(two, 4, 2), run(two, 10, 2)], 2)
            else:
                take(run(two, 0, 12), self.sem(s, 2))
                add_into(run(part, 0, 4), [run(two, 4 * k, 4) for k in range(3)], 4)
            for c in (2, 1, 3):
                self.go(s, 4, run(part, c, 1), run(three, c - 1, 1), axis, c)

        def third_in(self):
            take(run(self.parts[0], 0, 9 if self.index < 2 else 8), recv_sem.at[self.index, 12])

        def total(self, s):
            part, three = self.parts[s], self.threes[s]
            total = part[0].astype(jnp.float32)
            for c in range(3):
                total += three[c].astype(jnp.float32)
            return total

    chunks = {name: Chunk(at, name in RINGS) for at, name in enumerate(("q0", "q1", "k0", "k1"))}

    def store(pair, cuts, stride, s, i, term, lanes_from):
        xr, zr = i // 4, i % 4
        at, rows = cuts[s]
        for y in range(4):
            place = {"x": xr, "z": zr, "y": lax.rem(y - where["y"] + 4, 4)}
            place = sum(place[a] * w for a, w in zip(ORDERS[s], (16, 4, 1)))
            for half in range(2):
                lane = lanes_from + half * LANES
                chunks[pair[half]].parts[s][place] = term[
                    y * stride + at:y * stride + at + rows, lane:lane + LANES
                ]

    def slab_q(s, unit_of, count):
        for i in (unit_of(j) for j in range(count)):
            term = lax.dot_general(
                gq[i], lq[:, s * SLAB:(s + 1) * SLAB], (((0,), (0,)), ((), ())),
                preferred_element_type=jnp.float32,
            ).astype(jnp.bfloat16)
            store(("q0", "q1"), Q_CUT, Q_ROWS, s, i, term, 0)

    def unit_k(i):
        term = lax.dot_general(
            gk[i], lk[...], (((0,), (0,)), ((), ())), preferred_element_type=jnp.float32
        ).astype(jnp.bfloat16)
        for s in range(3):
            store(("k0", "k1"), KV_CUT, KV_ROWS, s, i, term, 0)

    def units_k(j, carry):
        many = gk.at[pl.ds(0, 4)]
        pltpu.make_async_copy(many, many, gk_sem.at[j]).wait()
        for i in range(4):
            unit_k(4 * j + i)
        return carry

    def each_q(act, *args):
        for name in ("q0", "q1"):
            getattr(chunks[name], act)(*args)

    big, small = chunks["q0"], chunks["q1"]
    load_lq[0].wait()
    need_q(0)
    slab_q(0, lambda j: 8 + j, 2)
    pl.semaphore_wait(barrier, len(friends))
    big.far(0, 0)
    need_q(1)
    slab_q(0, lambda j: 10 + j, 2)
    big.far(0, 1)
    load_lq[2].wait()
    slab_q(2, lambda j: 8 + j, 4)
    each_q("far_one", 2, 2)
    need_q(2)
    slab_q(2, lambda j: j, 4)
    each_q("far_one", 2, 0)
    load_lq[1].wait()
    need_q(3)
    slab_q(1, lambda j: 2 + 4 * j, 4)
    big.far(1, 0)
    big.far(1, 1)
    load_lk.start()
    start_k()
    for load in load_held:
        load.start()
    need_q(4)
    slab_q(0, lambda j: 6 + j, 2)
    big.near(0, 1)
    slab_q(0, lambda j: 12 + j, 2)
    big.near(0, 0)
    small.far(0, 0)
    small.far(0, 1)
    slab_q(2, lambda j: 12 + j, 4)
    big.far_one(2, 3)
    big.near(2, 1)
    slab_q(2, lambda j: 4 + j, 4)
    big.far_one(2, 1)
    big.near(2, 0)
    small.far_one(2, 3)
    small.far_one(2, 1)
    slab_q(1, lambda j: 1 + 4 * j, 4)
    big.near(1, 1)
    slab_q(1, lambda j: 3 + 4 * j, 4)
    big.near(1, 0)
    small.far(1, 0)
    small.far(1, 1)
    slab_q(0, lambda j: 4 + j, 2)
    slab_q(0, lambda j: 14 + j, 2)
    slab_q(0, lambda j: j, 4)
    slab_q(1, lambda j: 4 * j, 4)

    kinds = {
        "q": (sum_q, held_q, new_q, x_q, Q_ROWS, 3 * LANES),
        "k": (sum_k, held_k, new_k, x_k, KV_ROWS, LANES),
    }

    def slot(name, owner, c):
        _, _, _, x_ref, rows, cols = kinds[name[0]]
        return x_ref.at[
            pl.ds(pl.multiple_of(lax.rem(owner, 2) * rows, rows), rows),
            pl.ds(pl.multiple_of((c * 2 + int(name[1])) * cols, LANES), cols),
        ]

    def group_copy(name, k, block, way=None):
        index = chunks[name].index
        return pltpu.make_async_remote_copy(
            src_ref=block,
            dst_ref=block,
            send_sem=ag_send.at[index],
            recv_sem=ag_recv.at[index, 1 if k == 1 else 0],
            device_id=group[k if way is None else way],
            device_id_type=MESH,
        )

    def blocks(name, count):
        _, _, _, x_ref, rows, cols = kinds[name[0]]
        return x_ref.at[pl.ds(0, rows), pl.ds(0, count * cols)]

    def gather(name):
        total, held, new_ref, x_ref, rows, cols = kinds[name[0]]
        if name in ("q0", "k0"):
            load_held["kq".index(name[0])].wait()
        for t in range(cols // LANES):
            at = pl.ds((2 * t + int(name[1])) * LANES, LANES)
            gradient = total[:, at]
            renewed = momentum_rate * held[:, at] + gradient
            prepared = gradient + momentum_rate * renewed
            new_ref[:, at] = renewed
            part = pl.ds(
                pl.multiple_of((core * 2 + int(name[1])) * cols + t * LANES, LANES), LANES
            )
            x_ref[pl.ds(pl.multiple_of(low * rows, rows), rows), part] = prepared.astype(
                jnp.bfloat16
            )
        mine = slot(name, me, core)
        for k in (1, 0) if name in FORWARDED else (1, 2, 0):
            group_copy(name, k, mine).start()

    def forward(name):
        take(blocks(name, 1), ag_recv.at[chunks[name].index, 1])
        group_copy(name, 2, slot(name, *group[1]), 0).start()

    def end(name):
        if name not in FORWARDED:
            take(blocks(name, 1), ag_recv.at[chunks[name].index, 1])
        take(blocks(name, 2), ag_recv.at[chunks[name].index, 0])
        take(blocks(name, 3), ag_send.at[chunks[name].index])

    for item in PLAN:
        act, name = item.split()
        if act == "products":
            load_lk.wait()
            lax.fori_loop(0, 4, units_k, 0)
        elif act in ("far", "near"):
            for s in range(3):
                for half in range(2):
                    getattr(chunks[name], act)(s, half)
        elif act in ("relay1", "second", "relay2", "third"):
            for s in range(3):
                getattr(chunks[name], act)(s)
        elif act == "last":
            half = int(name[1])
            chunks[name].third_in()
            for s in range(3):
                total = chunks[name].total(s)
                if name[0] == "q":
                    lane = s * SLAB + half * LANES
                    sum_q[:, lane:lane + LANES] = total
                else:
                    at, rows = KV_CUT[s]
                    sum_k[at:at + rows, half * LANES:(half + 1) * LANES] = total
        elif act == "gather":
            gather(name)
        elif act == "forward":
            forward(name)
        elif act == "end":
            end(name)
    for chunk in chunks.values():
        chunk.sent()


def closing(
    prep_k, prep_q, new_k, new_q, out_uk, out_nk, out_uq, out_nq,
    x_k, x_q, mix_k, mix_q, up_k, up_q, sem,
):
    moves = ((new_k, out_nk), (new_q, out_nq), (up_k, out_uk), (up_q, out_uq))
    moves = [pltpu.make_async_copy(a, b, sem.at[k]) for k, (a, b) in enumerate(moves)]
    moves[0].start()
    moves[1].start()
    newton(((prep_k, x_k, mix_k, up_k), (prep_q, x_q, mix_q, up_q)))
    moves[2].start()
    moves[3].start()
    for move in moves:
        move.wait()


def per_device(latent_kv, latent_q, grad_kv, grad_q, momentum_kv, momentum_q):
    arrays = (latent_kv, latent_q, grad_kv, grad_q, momentum_kv, momentum_q)
    arrays = [pltpu.with_memory_space_constraint(array, pltpu.HBM) for array in arrays]
    low, full = jnp.bfloat16, jnp.float32
    cuts = (Q_CUT, Q_CUT, KV_CUT, KV_CUT)

    def cells(*lead):
        return [[pltpu.VMEM(lead + (rows, LANES), low) for _, rows in cut] for cut in cuts]

    vmem = pl.BlockSpec(memory_space=pltpu.VMEM)
    hbm = pl.BlockSpec(memory_space=pl.ANY)
    middle = pl.pallas_call(
        kernel,
        out_shape=(
            pltpu.VMEM((2 * KV_ROWS, 2 * KV_COLS), low),
            pltpu.VMEM((2 * Q_ROWS, 2 * Q_COLS), low),
            pltpu.VMEM((KV_ROWS, KV_COLS), full),
            pltpu.VMEM((Q_ROWS, Q_COLS), full),
        ),
        in_specs=[hbm] * 6,
        out_specs=(vmem,) * 4,
        scratch_shapes=[
            pltpu.VMEM((TOK, KV_COLS), low),
            pltpu.VMEM((TOK, Q_COLS), low),
            pltpu.VMEM((16, TOK, 4 * KV_ROWS), low),
            pltpu.VMEM((16, TOK, 4 * Q_ROWS), low),
            cells(64),
            cells(48),
            cells(12),
            cells(3),
            pltpu.VMEM((KV_ROWS, KV_COLS), full),
            pltpu.VMEM((Q_ROWS, Q_COLS), full),
            pltpu.VMEM((KV_ROWS, KV_COLS), full),
            pltpu.VMEM((Q_ROWS, Q_COLS), full),
            pltpu.SemaphoreType.DMA((6,)),
            pltpu.SemaphoreType.DMA((4,)),
            pltpu.SemaphoreType.DMA((5,)),
            pltpu.SemaphoreType.DMA((4, 3)),
            pltpu.SemaphoreType.DMA((4, 13)),
            pltpu.SemaphoreType.DMA((4,)),
            pltpu.SemaphoreType.DMA((4, 2)),
        ],
        compiler_params=pltpu.CompilerParams(
            collective_id=0, has_side_effects=True, vmem_limit_bytes=50 * 2**20
        ),
        name="sum_all",
    )(*arrays)
    return pl.pallas_call(
        closing,
        out_shape=(
            jax.ShapeDtypeStruct((KV_ROWS, KV_COLS), low),
            jax.ShapeDtypeStruct((KV_ROWS, KV_COLS), full),
            jax.ShapeDtypeStruct((Q_ROWS, Q_COLS), low),
            jax.ShapeDtypeStruct((Q_ROWS, Q_COLS), full),
        ),
        in_specs=[vmem] * 4,
        out_specs=(hbm,) * 4,
        scratch_shapes=[
            pltpu.VMEM((2 * KV_ROWS, 2 * KV_COLS), low),
            pltpu.VMEM((2 * Q_ROWS, 2 * Q_COLS), low),
            pltpu.VMEM((2 * KV_ROWS, 2 * KV_ROWS), low),
            pltpu.VMEM((2 * Q_ROWS, 2 * Q_ROWS), low),
            pltpu.VMEM((KV_ROWS, KV_COLS), low),
            pltpu.VMEM((Q_ROWS, Q_COLS), low),
            pltpu.SemaphoreType.DMA((4,)),
        ],
        compiler_params=pltpu.CompilerParams(vmem_limit_bytes=24 * 2**20),
        name="closing",
    )(*middle)


def solution(mesh):
    in_specs = (
        P("dp", "tensor"),
        P("dp", "tensor"),
        P("dp", None),
        P("dp", None),
        P("dp", "tensor"),
        P("dp", "tensor"),
    )
    out_specs = (P("dp", "tensor"), P("dp", "tensor"), P("dp", "tensor"), P("dp", "tensor"))
    return jax.shard_map(
        per_device, mesh=mesh, in_specs=in_specs, out_specs=out_specs, check_vma=False
    )
```

```python
import functools

import jax
import jax.numpy as jnp
from jax import lax
from jax.experimental import pallas as pl
from jax.experimental.pallas import tpu as pltpu
from jax.sharding import PartitionSpec as P

ITERS = 5
SIDE = 4
MESH = pl.DeviceIdType.MESH

first_coef = 3.4445
second_coef = -4.775
third_coef = 2.0315
momentum_rate = 0.95
norm_eps = 1e-07

TOK = 512
KV_ROWS, KV_COLS = 128, 256
Q_ROWS, Q_COLS = 96, 768
LANES = 128
SLAB = 2 * LANES
ORDERS = ("xzy", "zyx", "yxz")
KV_CUT = ((0, 48), (48, 48), (96, 32))
Q_CUT = ((0, 96),) * 3
FORWARDED = ("q0", "q1", "k0")
RINGS = ("q0", "q1", "k0")

Q0, Q1, K0, K1 = "q0", "q1", "k0", "k1"
PRODUCTS, OWN, FAR, NEAR, LAST, GATHER, FORWARD, END = range(8)
RELAY1, SECOND, RELAY2, THIRD = "relay1", "second", "relay2", "third"
PLAN = (
    (PRODUCTS, 3), (PRODUCTS, 1), (PRODUCTS, 2), (OWN, 1), (OWN, 0), (RELAY1, Q0, 1),
    (PRODUCTS, 0), (FAR, K0, 2), (FAR, K1, 0), (FAR, K1, 2), (FAR, K0, 0), (RELAY1, Q0, 0),
    (RELAY1, Q0, 2), (NEAR, K1, 0), (RELAY1, K1, 0), (NEAR, Q1, 1), (NEAR, Q1, 2),
    (RELAY1, Q1, 2), (NEAR, Q1, 0), (RELAY1, Q1, 0), (FAR, K0, 1), (NEAR, K0, 2), (RELAY1, K0, 2),
    (SECOND, Q0, 0), (RELAY1, Q1, 1), (SECOND, Q0, 2), (NEAR, K1, 2), (RELAY1, K1, 2),
    (SECOND, Q0, 1), (FAR, K1, 1), (NEAR, K0, 0), (RELAY1, K0, 0), (NEAR, K0, 1), (RELAY1, K0, 1),
    (SECOND, Q1, 2), (SECOND, Q1, 0), (SECOND, Q1, 1), (NEAR, K1, 1), (RELAY1, K1, 1),
    (RELAY2, Q0, 2), (RELAY2, Q0, 0), (SECOND, K0, 1), (RELAY2, Q1, 0), (RELAY2, Q1, 1),
    (SECOND, K0, 2), (RELAY2, Q0, 1), (RELAY2, Q1, 2), (RELAY2, K0, 1), (SECOND, K0, 0),
    (SECOND, K1, 2), (SECOND, K1, 0), (RELAY2, K0, 2), (SECOND, K1, 1), (THIRD, Q0, 2),
    (THIRD, Q1, 1), (THIRD, Q0, 0), (THIRD, Q0, 1), (RELAY2, K0, 0), (THIRD, Q1, 2),
    (THIRD, Q1, 0), (THIRD, K0, 1), (THIRD, K1, 1), (THIRD, K1, 0), (THIRD, K1, 2),
    (THIRD, K0, 0), (LAST, Q0), (GATHER, Q0), (LAST, Q1), (GATHER, Q1), (THIRD, K0, 2),
    (LAST, K0), (GATHER, K0), (LAST, K1), (GATHER, K1), (FORWARD, Q0), (END, Q0), (FORWARD, Q1),
    (END, Q1), (FORWARD, K0), (END, K0), (END, K1),
)


def shifted(where, axis, step):
    moved = dict(where)
    moved[axis] = lax.rem(moved[axis] + step + SIDE, SIDE)
    return (moved["x"] * SIDE + moved["z"]) * SIDE + moved["y"]


def gram_of(matrix):
    return lax.dot_general(
        matrix, matrix, (((1,), (1,)), ((), ())), preferred_element_type=jnp.float32
    )


def mixers(grams):
    lows = [gram.astype(jnp.bfloat16) for gram in grams]
    squares = [jnp.dot(low, low, preferred_element_type=jnp.float32) for low in lows]
    return [
        (second_coef * low.astype(jnp.float32) + third_coef * square).astype(jnp.bfloat16)
        for low, square in zip(lows, squares)
    ]


def advance(iterate, mixing, source, scale=None):
    moved = jnp.dot(mixing, source, preferred_element_type=jnp.float32)
    total = first_coef * iterate.astype(jnp.float32) + moved
    if scale is not None:
        total = total * scale
    return total.astype(jnp.bfloat16)


def scale_of(gram):
    at = [lax.broadcasted_iota(jnp.int32, gram.shape, d) for d in range(2)]
    squares = jnp.sum(jnp.where(at[0] == at[1], gram, 0.0), keepdims=True)
    return 1.0 / (jnp.sqrt(squares) + norm_eps)


def newton(heads):
    own_row, own_col = lax.rem(lax.axis_index("dp"), 2), lax.axis_index("tensor")
    for sweep in range(ITERS):
        source = [head[0] if sweep == 0 else head[1] for head in heads]
        wholes = [ref[...] for ref in source]
        grams = [gram_of(whole) for whole in wholes]
        scales = [None] * len(heads)
        if sweep == 0:
            scales = [scale_of(gram) for gram in grams]
            grams = [gram * scale * scale for gram, scale in zip(grams, scales)]
        mixings = mixers(grams)
        for head, whole, mixing, scale in zip(heads, wholes, mixings, scales):
            _, x_ref, mix_ref, out_ref = head
            if sweep < ITERS - 1:
                x_ref[...] = advance(whole, mixing, whole, scale)
                continue
            mix_ref[...] = mixing
            rows, cols = out_ref.shape
            own_rows = pl.ds(pl.multiple_of(own_row * rows, rows), rows)
            own_cols = pl.ds(pl.multiple_of(own_col * cols, cols), cols)
            own = advance(
                x_ref[own_rows, own_cols], mix_ref[own_rows, :], x_ref[:, own_cols]
            )
            slabs = cols // (2 * LANES)
            for at in range(2 * slabs):
                lane = (at % slabs * 2 + at // slabs) * LANES
                out_ref[:, lane:lane + LANES] = own[:, at * LANES:(at + 1) * LANES]


def add_into(target, others, count):
    def step(i, carry):
        total = target[i].astype(jnp.float32)
        for other in others:
            total += other[i].astype(jnp.float32)
        target[i] = total.astype(target.dtype)
        return carry

    lax.fori_loop(0, count, step, 0)


def kernel(
    lat_kv, lat_q, grad_kv, grad_q, mom_kv, mom_q,
    x_k, x_q, new_k, new_q,
    lk, lq, gk, gq, parts, ones, twos, threes, sum_k, sum_q, held_k, held_q,
    in_sem, gk_sem, gq_sem, send_sem, recv_sem, ag_send, ag_recv,
):
    me = lax.axis_index("dp")
    core = lax.axis_index("tensor")
    where = {"x": me // 16, "z": lax.rem(me // 4, 4), "y": lax.rem(me, 4)}
    low = lax.rem(me, 2)
    twin = me + 1 - 2 * low
    group = ((me, 1 - core), (twin, core), (twin, 1 - core))

    barrier = pltpu.get_barrier_semaphore()
    friends = [(shifted(where, a, s), core) for a in "xyz" for s in (1, 2, 3)]
    friends += [group[0], group[2]]
    for friend in friends:
        pl.semaphore_signal(barrier, inc=1, device_id=friend, device_id_type=MESH)

    def fetch(source, target, sem, width, i):
        u = lax.rem(where["x"] + i // 4, 4) * 4 + lax.rem(where["z"] + lax.rem(i, 4), 4)
        at = pl.multiple_of(u * width, 128)
        return pltpu.make_async_copy(source.at[:, pl.ds(at, width)], target.at[i], sem)

    q_sets = ((8, 9), (10, 11), (0, 1, 2, 3), (6, 14), (4, 5, 7, 12, 13, 15))

    def start_q(k):
        for i in q_sets[k]:
            fetch(grad_q, gq, gq_sem.at[k], 4 * Q_ROWS, i).start()

    def need_q(k):
        many = gq.at[pl.ds(0, len(q_sets[k]))]
        pltpu.make_async_copy(many, many, gq_sem.at[k]).wait()

    def start_k():
        for i in range(16):
            fetch(grad_kv, gk, gk_sem.at[i // 4], 4 * KV_ROWS, i).start()

    load_lq = [
        pltpu.make_async_copy(
            lat_q.at[:, pl.ds(k * SLAB, SLAB)], lq.at[:, pl.ds(k * SLAB, SLAB)], in_sem.at[k]
        )
        for k in range(3)
    ]
    load_lk = pltpu.make_async_copy(lat_kv, lk, in_sem.at[3])
    load_held = [
        pltpu.make_async_copy(mom_kv, held_k, in_sem.at[4]),
        pltpu.make_async_copy(mom_q, held_q, in_sem.at[5]),
    ]
    load_lq[0].start()
    start_q(0)
    start_q(1)
    load_lq[2].start()
    start_q(2)
    load_lq[1].start()
    start_q(3)
    start_q(4)

    ways = {(a, k): shifted(where, a, k) for a in "xyz" for k in (1, -1, 2, 3)}

    def take(ref, sem):
        pltpu.make_async_remote_copy(
            src_ref=ref, dst_ref=ref, send_sem=sem, recv_sem=sem,
            device_id=group[0], device_id_type=MESH,
        ).wait_recv()

    def run(ref, start, count):
        return ref.at[pl.ds(start, count)]

    class Chunk:
        def __init__(self, index, ring):
            self.index, self.ring = index, ring
            self.parts, self.ones = parts[index], ones[index]
            self.twos, self.threes = twos[index], threes[index]

        def sem(self, s, stage):
            return recv_sem.at[self.index, 4 * s + stage]

        def go(self, s, stage, source, target, axis, step):
            pltpu.make_async_remote_copy(
                src_ref=source,
                dst_ref=target,
                send_sem=send_sem.at[self.index, s],
                recv_sem=self.sem(s, stage) if stage < 4 else recv_sem.at[self.index, 12],
                device_id=(ways[axis, step], core),
                device_id_type=MESH,
            ).start()

        def sent(self):
            for s in range(3):
                take(run(self.parts[s], 0, 63), send_sem.at[self.index, s])

        def far(self, s, half):
            part, got, axis = self.parts[s], self.ones[s], ORDERS[s][0]
            step = 1 if half == 0 else -1
            self.go(s, 0, run(part, 32 + 8 * half, 8), run(got, 8 * half, 8), axis, step)

        def far_one(self, s, b):
            part, got, axis = self.parts[s], self.ones[s], ORDERS[s][0]
            step = 1 if b < 2 else -1
            self.go(s, 0, run(part, 32 + 4 * b, 4), run(got, 4 * b, 4), axis, step)

        def near(self, s, half):
            part, got, axis = self.parts[s], self.ones[s], ORDERS[s][0]
            if half == 0:
                self.go(s, 1, run(part, 48, 8), run(got, 24, 8), axis, -1)
            else:
                self.go(s, 1, run(part, 24, 8), run(got, 16, 8), axis, 1)

        def relay1(self, s):
            part, got, axis = self.parts[s], self.ones[s], ORDERS[s][0]
            take(run(got, 0, 16), self.sem(s, 0))
            add_into(run(part, 16, 8), [run(got, 0, 8)], 8)
            self.go(s, 1, run(part, 16, 8), run(got, 32, 8), axis, 1)
            add_into(run(part, 56, 8), [run(got, 8, 8)], 8)
            self.go(s, 1, run(part, 56, 8), run(got, 40, 8), axis, -1)

        def second(self, s):
            part, got, two, axis = self.parts[s], self.ones[s], self.twos[s], ORDERS[s][1]
            take(run(got, 16, 32), self.sem(s, 1))
            add_into(run(part, 8, 4), [run(got, 16, 4), run(got, 40, 4)], 4)
            if self.ring:
                self.go(s, 2, run(part, 8, 2), run(two, 0, 2), axis, 1)
                self.go(s, 2, run(part, 10, 2), run(two, 2, 2), axis, -1)
            else:
                self.go(s, 2, run(part, 8, 4), run(two, 4, 4), axis, 2)
            add_into(run(part, 12, 4), [run(got, 20, 4), run(got, 44, 4)], 4)
            if self.ring:
                self.go(s, 3, run(part, 12, 2), run(two, 6, 2), axis, -1)
            else:
                self.go(s, 2, run(part, 12, 4), run(two, 8, 4), axis, 3)
            add_into(run(part, 4, 4), [run(got, 28, 4), run(got, 36, 4)], 4)
            if self.ring:
                self.go(s, 3, run(part, 6, 2), run(two, 4, 2), axis, 1)
            else:
                self.go(s, 2, run(part, 4, 4), run(two, 0, 4), axis, 1)
            add_into(run(part, 0, 4), [run(got, 24, 4), run(got, 32, 4)], 4)

        def relay2(self, s):
            part, two, axis = self.parts[s], self.twos[s], ORDERS[s][1]
            take(run(two, 0, 4), self.sem(s, 2))
            add_into(run(part, 4, 2), [run(two, 0, 2)], 2)
            self.go(s, 3, run(part, 4, 2), run(two, 8, 2), axis, 1)
            add_into(run(part, 14, 2), [run(two, 2, 2)], 2)
            self.go(s, 3, run(part, 14, 2), run(two, 10, 2), axis, -1)

        def third(self, s):
            part, two, three, axis = self.parts[s], self.twos[s], self.threes[s], ORDERS[s][2]
            if self.ring:
                take(run(two, 4, 8), self.sem(s, 3))
                add_into(run(part, 0, 2), [run(two, 6, 2), run(two, 8, 2)], 2)
                add_into(run(part, 2, 2), [run(two, 4, 2), run(two, 10, 2)], 2)
            else:
                take(run(two, 0, 12), self.sem(s, 2))
                add_into(run(part, 0, 4), [run(two, 4 * k, 4) for k in range(3)], 4)
            for c in (2, 1, 3):
                self.go(s, 4, run(part, c, 1), run(three, c - 1, 1), axis, c)

        def third_in(self):
            take(run(self.parts[0], 0, 9 if self.index < 2 else 8), recv_sem.at[self.index, 12])

        def total(self, s):
            part, three = self.parts[s], self.threes[s]
            total = part[0].astype(jnp.float32)
            for c in range(3):
                total += three[c].astype(jnp.float32)
            return total

    chunks = {name: Chunk(at, name in RINGS) for at, name in enumerate(("q0", "q1", "k0", "k1"))}

    def store(pair, cuts, stride, s, i, term, lanes_from):
        xr, zr = i // 4, i % 4
        at, rows = cuts[s]
        for y in range(4):
            place = {"x": xr, "z": zr, "y": lax.rem(y - where["y"] + 4, 4)}
            place = sum(place[a] * w for a, w in zip(ORDERS[s], (16, 4, 1)))
            for half in range(2):
                lane = lanes_from + half * LANES
                chunks[pair[half]].parts[s][place] = term[
                    y * stride + at:y * stride + at + rows, lane:lane + LANES
                ]

    def slab_q(s, unit_of, count):
        for i in (unit_of(j) for j in range(count)):
            term = lax.dot_general(
                gq[i], lq[:, s * SLAB:(s + 1) * SLAB], (((0,), (0,)), ((), ())),
                preferred_element_type=jnp.float32,
            ).astype(jnp.bfloat16)
            store(("q0", "q1"), Q_CUT, Q_ROWS, s, i, term, 0)

    def unit_k(i):
        term = lax.dot_general(
            gk[i], lk[...], (((0,), (0,)), ((), ())), preferred_element_type=jnp.float32
        ).astype(jnp.bfloat16)
        for s in range(3):
            store(("k0", "k1"), KV_CUT, KV_ROWS, s, i, term, 0)

    def units_k(j):
        many = gk.at[pl.ds(0, 4)]
        pltpu.make_async_copy(many, many, gk_sem.at[j]).wait()
        for i in range(4):
            unit_k(4 * j + i)

    def each_q(act, *args):
        for name in ("q0", "q1"):
            getattr(chunks[name], act)(*args)

    big, small = chunks["q0"], chunks["q1"]
    load_lq[0].wait()
    need_q(0)
    slab_q(0, lambda j: 8 + j, 2)
    pl.semaphore_wait(barrier, len(friends))
    big.far(0, 0)
    need_q(1)
    slab_q(0, lambda j: 10 + j, 2)
    big.far(0, 1)
    load_lq[2].wait()
    slab_q(2, lambda j: 8 + j, 4)
    each_q("far_one", 2, 2)
    need_q(2)
    slab_q(2, lambda j: j, 4)
    each_q("far_one", 2, 0)
    load_lq[1].wait()
    need_q(3)
    slab_q(1, lambda j: 2 + 4 * j, 4)
    big.far(1, 0)
    big.far(1, 1)
    load_lk.start()
    start_k()
    for load in load_held:
        load.start()
    need_q(4)
    slab_q(0, lambda j: 6 + j, 2)
    big.near(0, 1)
    slab_q(0, lambda j: 12 + j, 2)
    big.near(0, 0)
    small.far(0, 0)
    small.far(0, 1)
    slab_q(2, lambda j: 12 + j, 4)
    big.far_one(2, 3)
    big.near(2, 1)
    slab_q(2, lambda j: 4 + j, 4)
    big.far_one(2, 1)
    big.near(2, 0)
    small.far_one(2, 3)
    small.far_one(2, 1)
    slab_q(1, lambda j: 1 + 4 * j, 4)
    big.near(1, 1)
    slab_q(1, lambda j: 3 + 4 * j, 4)
    big.near(1, 0)
    small.far(1, 0)
    small.far(1, 1)
    slab_q(0, lambda j: 4 + j, 2)
    slab_q(0, lambda j: 14 + j, 2)

    kinds = {
        "q": (sum_q, held_q, new_q, x_q, Q_ROWS, 3 * LANES),
        "k": (sum_k, held_k, new_k, x_k, KV_ROWS, LANES),
    }

    def slot(name, owner, c):
        _, _, _, x_ref, rows, cols = kinds[name[0]]
        return x_ref.at[
            pl.ds(pl.multiple_of(lax.rem(owner, 2) * rows, rows), rows),
            pl.ds(pl.multiple_of((c * 2 + int(name[1])) * cols, LANES), cols),
        ]

    def group_copy(name, k, block, way=None):
        index = chunks[name].index
        return pltpu.make_async_remote_copy(
            src_ref=block,
            dst_ref=block,
            send_sem=ag_send.at[index],
            recv_sem=ag_recv.at[index, 1 if k == 1 else 0],
            device_id=group[k if way is None else way],
            device_id_type=MESH,
        )

    def blocks(name, count):
        _, _, _, x_ref, rows, cols = kinds[name[0]]
        return x_ref.at[pl.ds(0, rows), pl.ds(0, count * cols)]

    def gather(name):
        total, held, new_ref, x_ref, rows, cols = kinds[name[0]]
        if name in ("q0", "k0"):
            load_held["kq".index(name[0])].wait()
        for t in range(cols // LANES):
            at = pl.ds((2 * t + int(name[1])) * LANES, LANES)
            gradient = total[:, at]
            renewed = momentum_rate * held[:, at] + gradient
            prepared = gradient + momentum_rate * renewed
            new_ref[:, at] = renewed
            part = pl.ds(
                pl.multiple_of((core * 2 + int(name[1])) * cols + t * LANES, LANES), LANES
            )
            x_ref[pl.ds(pl.multiple_of(low * rows, rows), rows), part] = prepared.astype(
                jnp.bfloat16
            )
        mine = slot(name, me, core)
        for k in (1, 0) if name in FORWARDED else (1, 2, 0):
            group_copy(name, k, mine).start()

    def forward(name):
        take(blocks(name, 1), ag_recv.at[chunks[name].index, 1])
        group_copy(name, 2, slot(name, *group[1]), 0).start()

    def end(name):
        if name not in FORWARDED:
            take(blocks(name, 1), ag_recv.at[chunks[name].index, 1])
        take(blocks(name, 2), ag_recv.at[chunks[name].index, 0])
        take(blocks(name, 3), ag_send.at[chunks[name].index])

    first_products = next(at for act, at, *_ in PLAN if act == PRODUCTS)
    for act, name, *at in PLAN:
        if act == PRODUCTS:
            if name == first_products:
                load_lk.wait()
            units_k(name)
        elif act == OWN:
            slab_q(name, (lambda j: j, lambda j: 4 * j)[name], 4)
        elif act in (FAR, NEAR):
            for s in at:
                for half in range(2):
                    (chunks[name].far if act == FAR else chunks[name].near)(s, half)
        elif act in (RELAY1, SECOND, RELAY2, THIRD):
            for s in at:
                getattr(chunks[name], act)(s)
        elif act == LAST:
            half = int(name[1])
            chunks[name].third_in()
            for s in range(3):
                total = chunks[name].total(s)
                if name[0] == "q":
                    lane = s * SLAB + half * LANES
                    sum_q[:, lane:lane + LANES] = total
                else:
                    at, rows = KV_CUT[s]
                    sum_k[at:at + rows, half * LANES:(half + 1) * LANES] = total
        elif act == GATHER:
            gather(name)
        elif act == FORWARD:
            forward(name)
        elif act == END:
            end(name)
    for chunk in chunks.values():
        chunk.sent()


def closing(
    prep_k, prep_q, new_k, new_q, out_uk, out_nk, out_uq, out_nq,
    x_k, x_q, mix_k, mix_q, up_k, up_q, sem,
):
    moves = ((new_k, out_nk), (new_q, out_nq), (up_k, out_uk), (up_q, out_uq))
    moves = [pltpu.make_async_copy(a, b, sem.at[k]) for k, (a, b) in enumerate(moves)]
    moves[0].start()
    moves[1].start()
    newton(((prep_k, x_k, mix_k, up_k), (prep_q, x_q, mix_q, up_q)))
    moves[2].start()
    moves[3].start()
    for move in moves:
        move.wait()


def per_device(latent_kv, latent_q, grad_kv, grad_q, momentum_kv, momentum_q):
    arrays = (latent_kv, latent_q, grad_kv, grad_q, momentum_kv, momentum_q)
    arrays = [pltpu.with_memory_space_constraint(array, pltpu.HBM) for array in arrays]
    low, full = jnp.bfloat16, jnp.float32
    cuts = (Q_CUT, Q_CUT, KV_CUT, KV_CUT)

    def cells(*lead):
        return [[pltpu.VMEM(lead + (rows, LANES), low) for _, rows in cut] for cut in cuts]

    vmem = pl.BlockSpec(memory_space=pltpu.VMEM)
    hbm = pl.BlockSpec(memory_space=pl.ANY)
    middle = pl.pallas_call(
        kernel,
        out_shape=(
            pltpu.VMEM((2 * KV_ROWS, 2 * KV_COLS), low),
            pltpu.VMEM((2 * Q_ROWS, 2 * Q_COLS), low),
            pltpu.VMEM((KV_ROWS, KV_COLS), full),
            pltpu.VMEM((Q_ROWS, Q_COLS), full),
        ),
        in_specs=[hbm] * 6,
        out_specs=(vmem,) * 4,
        scratch_shapes=[
            pltpu.VMEM((TOK, KV_COLS), low),
            pltpu.VMEM((TOK, Q_COLS), low),
            pltpu.VMEM((16, TOK, 4 * KV_ROWS), low),
            pltpu.VMEM((16, TOK, 4 * Q_ROWS), low),
            cells(64),
            cells(48),
            cells(12),
            cells(3),
            pltpu.VMEM((KV_ROWS, KV_COLS), full),
            pltpu.VMEM((Q_ROWS, Q_COLS), full),
            pltpu.VMEM((KV_ROWS, KV_COLS), full),
            pltpu.VMEM((Q_ROWS, Q_COLS), full),
            pltpu.SemaphoreType.DMA((6,)),
            pltpu.SemaphoreType.DMA((4,)),
            pltpu.SemaphoreType.DMA((5,)),
            pltpu.SemaphoreType.DMA((4, 3)),
            pltpu.SemaphoreType.DMA((4, 13)),
            pltpu.SemaphoreType.DMA((4,)),
            pltpu.SemaphoreType.DMA((4, 2)),
        ],
        compiler_params=pltpu.CompilerParams(
            collective_id=0, has_side_effects=True, vmem_limit_bytes=50 * 2**20
        ),
        name="sum_all",
    )(*arrays)
    return pl.pallas_call(
        closing,
        out_shape=(
            jax.ShapeDtypeStruct((KV_ROWS, KV_COLS), low),
            jax.ShapeDtypeStruct((KV_ROWS, KV_COLS), full),
            jax.ShapeDtypeStruct((Q_ROWS, Q_COLS), low),
            jax.ShapeDtypeStruct((Q_ROWS, Q_COLS), full),
        ),
        in_specs=[vmem] * 4,
        out_specs=(hbm,) * 4,
        scratch_shapes=[
            pltpu.VMEM((2 * KV_ROWS, 2 * KV_COLS), low),
            pltpu.VMEM((2 * Q_ROWS, 2 * Q_COLS), low),
            pltpu.VMEM((2 * KV_ROWS, 2 * KV_ROWS), low),
            pltpu.VMEM((2 * Q_ROWS, 2 * Q_ROWS), low),
            pltpu.VMEM((KV_ROWS, KV_COLS), low),
            pltpu.VMEM((Q_ROWS, Q_COLS), low),
            pltpu.SemaphoreType.DMA((4,)),
        ],
        compiler_params=pltpu.CompilerParams(vmem_limit_bytes=24 * 2**20),
        name="closing",
    )(*middle)


def solution(mesh):
    in_specs = (
        P("dp", "tensor"),
        P("dp", "tensor"),
        P("dp", None),
        P("dp", None),
        P("dp", "tensor"),
        P("dp", "tensor"),
    )
    out_specs = (P("dp", "tensor"), P("dp", "tensor"), P("dp", "tensor"), P("dp", "tensor"))
    return jax.shard_map(
        per_device, mesh=mesh, in_specs=in_specs, out_specs=out_specs, check_vma=False
    )
```

```python
import functools

import jax
import jax.numpy as jnp
from jax import lax
from jax.experimental import pallas as pl
from jax.experimental.pallas import tpu as pltpu
from jax.sharding import PartitionSpec as P

ITERS = 5
SIDE = 4
MESH = pl.DeviceIdType.MESH

first_coef = 3.4445
second_coef = -4.775
third_coef = 2.0315
momentum_rate = 0.95
norm_eps = 1e-07

TOK = 512
KV_ROWS, KV_COLS = 128, 256
Q_ROWS, Q_COLS = 96, 768
LANES = 128
SLAB = 2 * LANES
ORDERS = ("xzy", "zyx", "yxz")
KV_CUT = ((0, 48), (48, 48), (96, 32))
Q_CUT = ((0, 96),) * 3
FORWARDED = ("q0", "q1", "k0")
RINGS = ("q0", "q1", "k0")

Q0, Q1, K0, K1 = "q0", "q1", "k0", "k1"
PRODUCTS, OWN, FAR, NEAR, LAST, GATHER, FORWARD, END = range(8)
RELAY1, SECOND, RELAY2, THIRD = "relay1", "second", "relay2", "third"
PLAN = (
    (PRODUCTS, 3), (PRODUCTS, 1), (PRODUCTS, 2), (OWN, 1), (OWN, 0), (RELAY1, Q0, 1),
    (PRODUCTS, 0), (FAR, K0, 2), (FAR, K1, 0), (FAR, K1, 2), (FAR, K0, 0), (RELAY1, Q0, 0),
    (RELAY1, Q0, 2), (NEAR, K1, 0), (RELAY1, K1, 0), (NEAR, Q1, 1), (NEAR, Q1, 2),
    (RELAY1, Q1, 2), (NEAR, Q1, 0), (RELAY1, Q1, 0), (FAR, K0, 1), (NEAR, K0, 2), (RELAY1, K0, 2),
    (SECOND, Q0, 0), (RELAY1, Q1, 1), (SECOND, Q0, 2), (NEAR, K1, 2), (RELAY1, K1, 2),
    (SECOND, Q0, 1), (FAR, K1, 1), (NEAR, K0, 0), (RELAY1, K0, 0), (NEAR, K0, 1), (RELAY1, K0, 1),
    (SECOND, Q1, 2), (SECOND, Q1, 0), (SECOND, Q1, 1), (NEAR, K1, 1), (RELAY1, K1, 1),
    (RELAY2, Q0, 2), (RELAY2, Q0, 0), (SECOND, K0, 1), (RELAY2, Q1, 0), (RELAY2, Q1, 1),
    (SECOND, K0, 2), (RELAY2, Q0, 1), (RELAY2, Q1, 2), (RELAY2, K0, 1), (SECOND, K0, 0),
    (SECOND, K1, 2), (SECOND, K1, 0), (RELAY2, K0, 2), (SECOND, K1, 1), (THIRD, Q0, 2),
    (THIRD, Q1, 1), (THIRD, Q0, 0), (THIRD, Q0, 1), (RELAY2, K0, 0), (THIRD, Q1, 2),
    (THIRD, Q1, 0), (THIRD, K0, 1), (THIRD, K1, 1), (THIRD, K1, 0), (THIRD, K1, 2),
    (THIRD, K0, 0), (LAST, Q0), (GATHER, Q0), (LAST, Q1), (GATHER, Q1), (THIRD, K0, 2),
    (LAST, K0), (GATHER, K0), (LAST, K1), (GATHER, K1), (FORWARD, Q0), (END, Q0), (FORWARD, Q1),
    (END, Q1), (FORWARD, K0), (END, K0), (END, K1),
)


def shifted(where, axis, step):
    moved = dict(where)
    moved[axis] = lax.rem(moved[axis] + step + SIDE, SIDE)
    return (moved["x"] * SIDE + moved["z"]) * SIDE + moved["y"]


def gram_of(matrix):
    return lax.dot_general(
        matrix, matrix, (((1,), (1,)), ((), ())), preferred_element_type=jnp.float32
    )


def mixers(grams):
    lows = [gram.astype(jnp.bfloat16) for gram in grams]
    squares = [jnp.dot(low, low, preferred_element_type=jnp.float32) for low in lows]
    return [
        (second_coef * low.astype(jnp.float32) + third_coef * square).astype(jnp.bfloat16)
        for low, square in zip(lows, squares)
    ]


def advance(iterate, mixing, source, scale=None):
    moved = jnp.dot(mixing, source, preferred_element_type=jnp.float32)
    total = first_coef * iterate.astype(jnp.float32) + moved
    if scale is not None:
        total = total * scale
    return total.astype(jnp.bfloat16)


def scale_of(gram):
    at = [lax.broadcasted_iota(jnp.int32, gram.shape, d) for d in range(2)]
    squares = jnp.sum(jnp.where(at[0] == at[1], gram, 0.0), keepdims=True)
    return 1.0 / (jnp.sqrt(squares) + norm_eps)


def newton(heads):
    own_row, own_col = lax.rem(lax.axis_index("dp"), 2), lax.axis_index("tensor")
    for sweep in range(ITERS):
        source = [head[0] if sweep == 0 else head[1] for head in heads]
        wholes = [ref[...] for ref in source]
        grams = [gram_of(whole) for whole in wholes]
        scales = [None] * len(heads)
        if sweep == 0:
            scales = [scale_of(gram) for gram in grams]
            grams = [gram * scale * scale for gram, scale in zip(grams, scales)]
        mixings = mixers(grams)
        for head, whole, mixing, scale in zip(heads, wholes, mixings, scales):
            _, x_ref, mix_ref, out_ref = head
            if sweep < ITERS - 1:
                x_ref[...] = advance(whole, mixing, whole, scale)
                continue
            mix_ref[...] = mixing
            rows, cols = out_ref.shape
            own_rows = pl.ds(pl.multiple_of(own_row * rows, rows), rows)
            own_cols = pl.ds(pl.multiple_of(own_col * cols, cols), cols)
            own = advance(
                x_ref[own_rows, own_cols], mix_ref[own_rows, :], x_ref[:, own_cols]
            )
            slabs = cols // (2 * LANES)
            for at in range(2 * slabs):
                lane = (at % slabs * 2 + at // slabs) * LANES
                out_ref[:, lane:lane + LANES] = own[:, at * LANES:(at + 1) * LANES]


def add_into(target, others, count):
    def step(i, carry):
        total = target[i].astype(jnp.float32)
        for other in others:
            total += other[i].astype(jnp.float32)
        target[i] = total.astype(target.dtype)
        return carry

    lax.fori_loop(0, count, step, 0)


def kernel(
    lat_kv, lat_q, grad_kv, grad_q, mom_kv, mom_q,
    x_k, x_q, new_k, new_q,
    lk, lq, gk, gq, parts, ones, twos, threes, sum_k, sum_q, held_k, held_q,
    in_sem, gk_sem, gq_sem, send_sem, recv_sem, ag_send, ag_recv,
):
    me = lax.axis_index("dp")
    core = lax.axis_index("tensor")
    where = {"x": me // 16, "z": lax.rem(me // 4, 4), "y": lax.rem(me, 4)}
    low = lax.rem(me, 2)
    twin = me + 1 - 2 * low
    group = ((me, 1 - core), (twin, core), (twin, 1 - core))

    barrier = pltpu.get_barrier_semaphore()
    friends = [(shifted(where, a, s), core) for a in "xyz" for s in (1, 2, 3)]
    friends += [group[0], group[2]]
    for friend in friends:
        pl.semaphore_signal(barrier, inc=1, device_id=friend, device_id_type=MESH)

    def fetch(source, target, sem, width, i):
        u = lax.rem(where["x"] + i // 4, 4) * 4 + lax.rem(where["z"] + lax.rem(i, 4), 4)
        at = pl.multiple_of(u * width, 128)
        return pltpu.make_async_copy(source.at[:, pl.ds(at, width)], target.at[i], sem)

    q_sets = ((8, 9), (10, 11), (0, 1, 2, 3), (6, 14), (4, 5, 7, 12, 13, 15))

    def start_q(k):
        for i in q_sets[k]:
            fetch(grad_q, gq, gq_sem.at[k], 4 * Q_ROWS, i).start()

    def need_q(k):
        many = gq.at[pl.ds(0, len(q_sets[k]))]
        pltpu.make_async_copy(many, many, gq_sem.at[k]).wait()

    def start_k():
        for i in range(16):
            fetch(grad_kv, gk, gk_sem.at[i // 4], 4 * KV_ROWS, i).start()

    load_lq = [
        pltpu.make_async_copy(
            lat_q.at[:, pl.ds(k * SLAB, SLAB)], lq.at[:, pl.ds(k * SLAB, SLAB)], in_sem.at[k]
        )
        for k in range(3)
    ]
    load_lk = pltpu.make_async_copy(lat_kv, lk, in_sem.at[3])
    load_held = [
        pltpu.make_async_copy(mom_kv, held_k, in_sem.at[4]),
        pltpu.make_async_copy(mom_q, held_q, in_sem.at[5]),
    ]
    load_lq[0].start()
    start_q(0)
    start_q(1)
    load_lq[2].start()
    start_q(2)
    load_lq[1].start()
    start_q(3)
    start_q(4)

    ways = {(a, k): shifted(where, a, k) for a in "xyz" for k in (1, -1, 2, 3)}

    def take(ref, sem):
        pltpu.make_async_remote_copy(
            src_ref=ref, dst_ref=ref, send_sem=sem, recv_sem=sem,
            device_id=group[0], device_id_type=MESH,
        ).wait_recv()

    def run(ref, start, count):
        return ref.at[pl.ds(start, count)]

    class Chunk:
        def __init__(self, index, ring):
            self.index, self.ring = index, ring
            self.parts, self.ones = parts[index], ones[index]
            self.twos, self.threes = twos[index], threes[index]

        def sem(self, s, stage):
            return recv_sem.at[self.index, 4 * s + stage]

        def go(self, s, stage, source, target, axis, step):
            pltpu.make_async_remote_copy(
                src_ref=source,
                dst_ref=target,
                send_sem=send_sem.at[self.index],
                recv_sem=self.sem(s, stage) if stage < 4 else recv_sem.at[self.index, 12],
                device_id=(ways[axis, step], core),
                device_id_type=MESH,
            ).start()

        def sent(self):
            units, rows, width = (14, 432, 384) if self.index < 2 else (7, 288, 512)
            many = gk.at[pl.ds(0, units), pl.ds(0, rows), pl.ds(0, width)]
            take(many, send_sem.at[self.index])

        def far(self, s, half):
            part, got, axis = self.parts[s], self.ones[s], ORDERS[s][0]
            step = 1 if half == 0 else -1
            self.go(s, 0, run(part, 32 + 8 * half, 8), run(got, 8 * half, 8), axis, step)

        def far_one(self, s, b):
            part, got, axis = self.parts[s], self.ones[s], ORDERS[s][0]
            step = 1 if b < 2 else -1
            self.go(s, 0, run(part, 32 + 4 * b, 4), run(got, 4 * b, 4), axis, step)

        def near(self, s, half):
            part, got, axis = self.parts[s], self.ones[s], ORDERS[s][0]
            if half == 0:
                self.go(s, 1, run(part, 48, 8), run(got, 24, 8), axis, -1)
            else:
                self.go(s, 1, run(part, 24, 8), run(got, 16, 8), axis, 1)

        def relay1(self, s):
            part, got, axis = self.parts[s], self.ones[s], ORDERS[s][0]
            take(run(got, 0, 16), self.sem(s, 0))
            add_into(run(part, 16, 8), [run(got, 0, 8)], 8)
            self.go(s, 1, run(part, 16, 8), run(got, 32, 8), axis, 1)
            add_into(run(part, 56, 8), [run(got, 8, 8)], 8)
            self.go(s, 1, run(part, 56, 8), run(got, 40, 8), axis, -1)

        def second(self, s):
            part, got, two, axis = self.parts[s], self.ones[s], self.twos[s], ORDERS[s][1]
            take(run(got, 16, 32), self.sem(s, 1))
            add_into(run(part, 8, 4), [run(got, 16, 4), run(got, 40, 4)], 4)
            if self.ring:
                self.go(s, 2, run(part, 8, 2), run(two, 0, 2), axis, 1)
                self.go(s, 2, run(part, 10, 2), run(two, 2, 2), axis, -1)
            else:
                self.go(s, 2, run(part, 8, 4), run(two, 4, 4), axis, 2)
            add_into(run(part, 12, 4), [run(got, 20, 4), run(got, 44, 4)], 4)
            if self.ring:
                self.go(s, 3, run(part, 12, 2), run(two, 6, 2), axis, -1)
            else:
                self.go(s, 2, run(part, 12, 4), run(two, 8, 4), axis, 3)
            add_into(run(part, 4, 4), [run(got, 28, 4), run(got, 36, 4)], 4)
            if self.ring:
                self.go(s, 3, run(part, 6, 2), run(two, 4, 2), axis, 1)
            else:
                self.go(s, 2, run(part, 4, 4), run(two, 0, 4), axis, 1)
            add_into(run(part, 0, 4), [run(got, 24, 4), run(got, 32, 4)], 4)

        def relay2(self, s):
            part, two, axis = self.parts[s], self.twos[s], ORDERS[s][1]
            take(run(two, 0, 4), self.sem(s, 2))
            add_into(run(part, 4, 2), [run(two, 0, 2)], 2)
            self.go(s, 3, run(part, 4, 2), run(two, 8, 2), axis, 1)
            add_into(run(part, 14, 2), [run(two, 2, 2)], 2)
            self.go(s, 3, run(part, 14, 2), run(two, 10, 2), axis, -1)

        def third(self, s):
            part, two, three, axis = self.parts[s], self.twos[s], self.threes[s], ORDERS[s][2]
            if self.ring:
                take(run(two, 4, 8), self.sem(s, 3))
                add_into(run(part, 0, 2), [run(two, 6, 2), run(two, 8, 2)], 2)
                add_into(run(part, 2, 2), [run(two, 4, 2), run(two, 10, 2)], 2)
            else:
                take(run(two, 0, 12), self.sem(s, 2))
                add_into(run(part, 0, 4), [run(two, 4 * k, 4) for k in range(3)], 4)
            for c in (2, 1, 3):
                self.go(s, 4, run(part, c, 1), run(three, c - 1, 1), axis, c)

        def third_in(self):
            take(run(self.parts[0], 0, 9 if self.index < 2 else 8), recv_sem.at[self.index, 12])

        def total(self, s):
            part, three = self.parts[s], self.threes[s]
            total = part[0].astype(jnp.float32)
            for c in range(3):
                total += three[c].astype(jnp.float32)
            return total

    chunks = {name: Chunk(at, name in RINGS) for at, name in enumerate(("q0", "q1", "k0", "k1"))}

    def store(pair, cuts, stride, s, i, term, lanes_from):
        xr, zr = i // 4, i % 4
        at, rows = cuts[s]
        for y in range(4):
            place = {"x": xr, "z": zr, "y": lax.rem(y - where["y"] + 4, 4)}
            place = sum(place[a] * w for a, w in zip(ORDERS[s], (16, 4, 1)))
            for half in range(2):
                lane = lanes_from + half * LANES
                chunks[pair[half]].parts[s][place] = term[
                    y * stride + at:y * stride + at + rows, lane:lane + LANES
                ]

    def slab_q(s, unit_of, count):
        for i in (unit_of(j) for j in range(count)):
            term = lax.dot_general(
                gq[i], lq[:, s * SLAB:(s + 1) * SLAB], (((0,), (0,)), ((), ())),
                preferred_element_type=jnp.float32,
            ).astype(jnp.bfloat16)
            store(("q0", "q1"), Q_CUT, Q_ROWS, s, i, term, 0)

    def unit_k(i):
        term = lax.dot_general(
            gk[i], lk[...], (((0,), (0,)), ((), ())), preferred_element_type=jnp.float32
        ).astype(jnp.bfloat16)
        for s in range(3):
            store(("k0", "k1"), KV_CUT, KV_ROWS, s, i, term, 0)

    def units_k(j):
        many = gk.at[pl.ds(0, 4)]
        pltpu.make_async_copy(many, many, gk_sem.at[j]).wait()
        for i in range(4):
            unit_k(4 * j + i)

    def each_q(act, *args):
        for name in ("q0", "q1"):
            getattr(chunks[name], act)(*args)

    big, small = chunks["q0"], chunks["q1"]
    load_lq[0].wait()
    need_q(0)
    slab_q(0, lambda j: 8 + j, 2)
    pl.semaphore_wait(barrier, len(friends))
    big.far(0, 0)
    need_q(1)
    slab_q(0, lambda j: 10 + j, 2)
    big.far(0, 1)
    load_lq[2].wait()
    slab_q(2, lambda j: 8 + j, 4)
    each_q("far_one", 2, 2)
    need_q(2)
    slab_q(2, lambda j: j, 4)
    each_q("far_one", 2, 0)
    load_lq[1].wait()
    need_q(3)
    slab_q(1, lambda j: 2 + 4 * j, 4)
    big.far(1, 0)
    big.far(1, 1)
    load_lk.start()
    start_k()
    for load in load_held:
        load.start()
    need_q(4)
    slab_q(0, lambda j: 6 + j, 2)
    big.near(0, 1)
    slab_q(0, lambda j: 12 + j, 2)
    big.near(0, 0)
    small.far(0, 0)
    small.far(0, 1)
    slab_q(2, lambda j: 12 + j, 4)
    big.far_one(2, 3)
    big.near(2, 1)
    slab_q(2, lambda j: 4 + j, 4)
    big.far_one(2, 1)
    big.near(2, 0)
    small.far_one(2, 3)
    small.far_one(2, 1)
    slab_q(1, lambda j: 1 + 4 * j, 4)
    big.near(1, 1)
    slab_q(1, lambda j: 3 + 4 * j, 4)
    big.near(1, 0)
    small.far(1, 0)
    small.far(1, 1)
    slab_q(0, lambda j: 4 + j, 2)
    slab_q(0, lambda j: 14 + j, 2)

    kinds = {
        "q": (sum_q, held_q, new_q, x_q, Q_ROWS, 3 * LANES),
        "k": (sum_k, held_k, new_k, x_k, KV_ROWS, LANES),
    }

    def slot(name, owner, c):
        _, _, _, x_ref, rows, cols = kinds[name[0]]
        return x_ref.at[
            pl.ds(pl.multiple_of(lax.rem(owner, 2) * rows, rows), rows),
            pl.ds(pl.multiple_of((c * 2 + int(name[1])) * cols, LANES), cols),
        ]

    def group_copy(name, k, block, way=None):
        index = chunks[name].index
        return pltpu.make_async_remote_copy(
            src_ref=block,
            dst_ref=block,
            send_sem=ag_send.at[index],
            recv_sem=ag_recv.at[index, 1 if k == 1 else 0],
            device_id=group[k if way is None else way],
            device_id_type=MESH,
        )

    def blocks(name, count):
        _, _, _, x_ref, rows, cols = kinds[name[0]]
        return x_ref.at[pl.ds(0, rows), pl.ds(0, count * cols)]

    def gather(name):
        total, held, new_ref, x_ref, rows, cols = kinds[name[0]]
        if name in ("q0", "k0"):
            load_held["kq".index(name[0])].wait()
        for t in range(cols // LANES):
            at = pl.ds((2 * t + int(name[1])) * LANES, LANES)
            gradient = total[:, at]
            renewed = momentum_rate * held[:, at] + gradient
            prepared = gradient + momentum_rate * renewed
            new_ref[:, at] = renewed
            part = pl.ds(
                pl.multiple_of((core * 2 + int(name[1])) * cols + t * LANES, LANES), LANES
            )
            x_ref[pl.ds(pl.multiple_of(low * rows, rows), rows), part] = prepared.astype(
                jnp.bfloat16
            )
        mine = slot(name, me, core)
        for k in (1, 0) if name in FORWARDED else (1, 2, 0):
            group_copy(name, k, mine).start()

    def forward(name):
        take(blocks(name, 1), ag_recv.at[chunks[name].index, 1])
        group_copy(name, 2, slot(name, *group[1]), 0).start()

    def end(name):
        if name not in FORWARDED:
            take(blocks(name, 1), ag_recv.at[chunks[name].index, 1])
        take(blocks(name, 2), ag_recv.at[chunks[name].index, 0])
        take(blocks(name, 3), ag_send.at[chunks[name].index])

    first_products = next(at for act, at, *_ in PLAN if act == PRODUCTS)
    for act, name, *at in PLAN:
        if act == PRODUCTS:
            if name == first_products:
                load_lk.wait()
            units_k(name)
        elif act == OWN:
            slab_q(name, (lambda j: j, lambda j: 4 * j)[name], 4)
        elif act in (FAR, NEAR):
            for s in at:
                for half in range(2):
                    (chunks[name].far if act == FAR else chunks[name].near)(s, half)
        elif act in (RELAY1, SECOND, RELAY2, THIRD):
            for s in at:
                getattr(chunks[name], act)(s)
        elif act == LAST:
            half = int(name[1])
            chunks[name].third_in()
            for s in range(3):
                total = chunks[name].total(s)
                if name[0] == "q":
                    lane = s * SLAB + half * LANES
                    sum_q[:, lane:lane + LANES] = total
                else:
                    at, rows = KV_CUT[s]
                    sum_k[at:at + rows, half * LANES:(half + 1) * LANES] = total
        elif act == GATHER:
            gather(name)
        elif act == FORWARD:
            forward(name)
        elif act == END:
            end(name)
    for chunk in chunks.values():
        chunk.sent()


def closing(
    prep_k, prep_q, new_k, new_q, out_uk, out_nk, out_uq, out_nq,
    x_k, x_q, mix_k, mix_q, up_k, up_q, sem,
):
    moves = ((new_k, out_nk), (new_q, out_nq), (up_k, out_uk), (up_q, out_uq))
    moves = [pltpu.make_async_copy(a, b, sem.at[k]) for k, (a, b) in enumerate(moves)]
    moves[0].start()
    moves[1].start()
    newton(((prep_k, x_k, mix_k, up_k), (prep_q, x_q, mix_q, up_q)))
    moves[2].start()
    moves[3].start()
    for move in moves:
        move.wait()


def per_device(latent_kv, latent_q, grad_kv, grad_q, momentum_kv, momentum_q):
    arrays = (latent_kv, latent_q, grad_kv, grad_q, momentum_kv, momentum_q)
    arrays = [pltpu.with_memory_space_constraint(array, pltpu.HBM) for array in arrays]
    low, full = jnp.bfloat16, jnp.float32
    cuts = (Q_CUT, Q_CUT, KV_CUT, KV_CUT)

    def cells(*lead):
        return [[pltpu.VMEM(lead + (rows, LANES), low) for _, rows in cut] for cut in cuts]

    vmem = pl.BlockSpec(memory_space=pltpu.VMEM)
    hbm = pl.BlockSpec(memory_space=pl.ANY)
    middle = pl.pallas_call(
        kernel,
        out_shape=(
            pltpu.VMEM((2 * KV_ROWS, 2 * KV_COLS), low),
            pltpu.VMEM((2 * Q_ROWS, 2 * Q_COLS), low),
            pltpu.VMEM((KV_ROWS, KV_COLS), full),
            pltpu.VMEM((Q_ROWS, Q_COLS), full),
        ),
        in_specs=[hbm] * 6,
        out_specs=(vmem,) * 4,
        scratch_shapes=[
            pltpu.VMEM((TOK, KV_COLS), low),
            pltpu.VMEM((TOK, Q_COLS), low),
            pltpu.VMEM((16, TOK, 4 * KV_ROWS), low),
            pltpu.VMEM((16, TOK, 4 * Q_ROWS), low),
            cells(64),
            cells(48),
            cells(12),
            cells(3),
            pltpu.VMEM((KV_ROWS, KV_COLS), full),
            pltpu.VMEM((Q_ROWS, Q_COLS), full),
            pltpu.VMEM((KV_ROWS, KV_COLS), full),
            pltpu.VMEM((Q_ROWS, Q_COLS), full),
            pltpu.SemaphoreType.DMA((6,)),
            pltpu.SemaphoreType.DMA((4,)),
            pltpu.SemaphoreType.DMA((5,)),
            pltpu.SemaphoreType.DMA((4,)),
            pltpu.SemaphoreType.DMA((4, 13)),
            pltpu.SemaphoreType.DMA((4,)),
            pltpu.SemaphoreType.DMA((4, 2)),
        ],
        compiler_params=pltpu.CompilerParams(
            collective_id=0, has_side_effects=True, vmem_limit_bytes=50 * 2**20
        ),
        name="sum_all",
    )(*arrays)
    return pl.pallas_call(
        closing,
        out_shape=(
            jax.ShapeDtypeStruct((KV_ROWS, KV_COLS), low),
            jax.ShapeDtypeStruct((KV_ROWS, KV_COLS), full),
            jax.ShapeDtypeStruct((Q_ROWS, Q_COLS), low),
            jax.ShapeDtypeStruct((Q_ROWS, Q_COLS), full),
        ),
        in_specs=[vmem] * 4,
        out_specs=(hbm,) * 4,
        scratch_shapes=[
            pltpu.VMEM((2 * KV_ROWS, 2 * KV_COLS), low),
            pltpu.VMEM((2 * Q_ROWS, 2 * Q_COLS), low),
            pltpu.VMEM((2 * KV_ROWS, 2 * KV_ROWS), low),
            pltpu.VMEM((2 * Q_ROWS, 2 * Q_ROWS), low),
            pltpu.VMEM((KV_ROWS, KV_COLS), low),
            pltpu.VMEM((Q_ROWS, Q_COLS), low),
            pltpu.SemaphoreType.DMA((4,)),
        ],
        compiler_params=pltpu.CompilerParams(vmem_limit_bytes=24 * 2**20),
        name="closing",
    )(*middle)


def solution(mesh):
    in_specs = (
        P("dp", "tensor"),
        P("dp", "tensor"),
        P("dp", None),
        P("dp", None),
        P("dp", "tensor"),
        P("dp", "tensor"),
    )
    out_specs = (P("dp", "tensor"), P("dp", "tensor"), P("dp", "tensor"), P("dp", "tensor"))
    return jax.shard_map(
        per_device, mesh=mesh, in_specs=in_specs, out_specs=out_specs, check_vma=False
    )
```
